256 devices in a mesh: segment: 4 (over x), dp: 8 (over z), tensor: 8 (over y, core).
Axes of the slice: x: 4, y: 4, z: 8, core: 2. Of those that a mesh axis runs over, the one named last changes fastest.
Arguments:
- inputs: bfloat16 [1, 64, 7168], P(None, ('dp', 'tensor')), may hold values from -6 to 6
- exit_at: int32 [1, 64], replicated, may hold values from 0 to 2
- targets: int32 [1, 64], replicated, may hold values from 0 to 25599
- repack: int32 [1, 2, 64], replicated, may hold values from 0 to 63, each once within a row
- norm_gain: float32 [4, 7168], P('segment'), may hold values from 0.5 to 1.5
- up_weight: bfloat16 [4, 14336, 7168], P('segment', ('dp', 'tensor')), may hold values from -0.0625 to 0.0625
- down_weight: bfloat16 [4, 14336, 7168], P('segment', ('dp', 'tensor')), may hold values from -0.046875 to 0.046875
- exit_gain: float32 [7168], replicated, may hold values from 0.5 to 1.5
- head: bfloat16 [25600, 7168], P(('dp', 'tensor')), may hold values from -0.21875 to 0.21875
Outputs:
- section_out: bfloat16 [4, 1, 64, 7168], P('segment', None, ('dp', 'tensor'))
- exit_logprob: float32 [1, 64], P(None, ('dp', 'tensor'))
The draws below stay inside these ranges and needn't reach their ends.
Inputs may be any that keep to these rules, and one draw needn't show every extreme that they name: Each repack[m, k] is a permutation of the 64 positions.
All inputs are finite; a program needn't handle non-finite values.
Results may differ from the reference program's by a relative error of at most 0.015.
Values may be sent and summed in bfloat16 or wider, within the bound.
No kernel may reach another device: no remote copies, remote signals or barrier semaphores. Data moves between devices by JAX's collectives and lax.ppermute only.
A program may use at most 64 MiB of HBM per device.

```python
import jax
import jax.numpy as jnp
from jax import lax

D = 7168
FFW = 14336
VOCW = 25600
MB = 1
ROWS = 64
N_SEGMENT = 4


def place_ends(values, stream_key, least, top_value):
    longest = values.shape.index(max(values.shape))
    spots = []
    for shift in (0, 1):
        where = [jax.random.randint(jax.random.fold_in(stream_key, axis), (), 0, length) for axis, length in enumerate(values.shape)]
        where[longest] = (where[longest] + shift) % values.shape[longest]
        spots.append(tuple(where))
    return values.at[spots[0]].set(least).at[spots[1]].set(top_value)


def block_scale(own_key, shape, cuts, low, largest):
    level, own = 1.0, jax.random.fold_in(own_key, 6)
    for axis_at, shards_of in cuts:
        draws = jnp.exp(jax.random.uniform(jax.random.fold_in(own, axis_at), (shards_of,), jnp.float32, low / len(cuts), largest / len(cuts)))
        level = level * jnp.repeat(draws, shape[axis_at] // shards_of).reshape([-1 if axis == axis_at else 1 for axis in range(len(shape))])
    return level


def gaussian(key, dims, scale, bound, cuts=(), kind=jnp.bfloat16):
    factor_of = block_scale(key, dims, cuts, -0.22, 0.18) if cuts else 1.0
    drawn = jax.random.normal(key, dims, jnp.float32) * scale * factor_of
    return jnp.minimum(jnp.maximum(drawn, -bound), bound).astype(kind)


def setup_inputs(seed: int = 0) -> dict:
    streams_of = jax.random.split(jax.random.key(seed), 10)
    inputs = gaussian(streams_of[0], (MB, ROWS, D), 1.0, 6.0, ((1, 64),))
    exit_at = place_ends(jax.random.randint(streams_of[1], (MB, ROWS), 0, 3), jax.random.fold_in(streams_of[1], 1), 0, 2).astype(jnp.int32)
    targets = place_ends(jax.random.randint(streams_of[2], (MB, ROWS), 0, VOCW), jax.random.fold_in(streams_of[2], 1), 0, VOCW - 1).astype(jnp.int32)
    repack = jax.vmap(lambda own: jax.random.permutation(own, ROWS))(jax.random.split(streams_of[3], MB * 2)).reshape((MB, 2, ROWS)).astype(jnp.int32)
    norm_gain = jnp.clip(1.0 + 0.1 * jax.random.normal(streams_of[4], (N_SEGMENT, D), jnp.float32), 0.5, 1.5)
    up_weight = gaussian(streams_of[5], (N_SEGMENT, FFW, D), D ** -0.5, 0.0625, ((0, 4), (1, 64)))
    down_weight = gaussian(streams_of[6], (N_SEGMENT, FFW, D), FFW ** -0.5, 0.046875, ((0, 4), (1, 64)))
    exit_gain = jnp.clip(1.0 + 0.1 * jax.random.normal(streams_of[7], (D,), jnp.float32), 0.5, 1.5)
    head = gaussian(streams_of[8], (VOCW, D), (D // 9) ** -0.5, 0.21875, ((0, 64),))
    return dict(inputs=inputs, exit_at=exit_at, targets=targets, repack=repack, norm_gain=norm_gain, up_weight=up_weight, down_weight=down_weight, exit_gain=exit_gain, head=head)


EPSILON = 1e-05

def layer_norm(buffer, scale):
    values = buffer.astype(jnp.float32)
    center = values - lax.optimization_barrier(jnp.mean(values, axis=-1, keepdims=True))
    spread = lax.optimization_barrier(jnp.mean(center * center, axis=-1, keepdims=True))
    return center * lax.rsqrt(spread + EPSILON) * scale

def contract(left, right):
    return lax.dot_general(left, right, (((1,), (1,)), ((), ())), preferred_element_type=jnp.float32)

def feed_forward(buffer, scale, up_matrix, down_matrix):
    normed = layer_norm(buffer, scale).astype(jnp.bfloat16)
    hidden = jax.nn.gelu(contract(normed, up_matrix), approximate=False).astype(jnp.bfloat16)
    summed = jnp.dot(hidden, down_matrix, preferred_element_type=jnp.float32)
    return (buffer.astype(jnp.float32) + summed).astype(jnp.bfloat16)

def exit_score(buffer, scale, head, wanted):
    normed = layer_norm(buffer, scale).astype(jnp.bfloat16)
    logits = contract(normed, head)
    exp_total = lax.optimization_barrier(jnp.sum(jnp.exp(logits), axis=1))
    picked = jnp.take_along_axis(logits, wanted[:, None], axis=1)[:, 0]
    return picked - jnp.log(exp_total)

def reference(inputs, exit_at, targets, repack, norm_gain, up_weight, down_weight, exit_gain, head):
    positions = jnp.arange(ROWS, dtype=jnp.int32)
    outputs = []
    scores = []
    for batch in range(MB):
        leaving = exit_at[batch]
        anchor = positions
        buffer = inputs[batch]
        found = jnp.zeros((ROWS,), jnp.float32)
        planes = []
        for section in range(N_SEGMENT):
            if section in (1, 2):
                scored = exit_score(buffer, exit_gain, head, targets[batch][anchor])
                chosen = leaving[anchor] == section
                found = found.at[anchor].add(jnp.where(chosen, scored, jnp.zeros_like(scored)))
                source = repack[batch, section - 1]
                anchor = anchor[source]
                buffer = buffer[source]
            exit_rank = leaving[anchor]
            living = (exit_rank == 0) | (exit_rank > section)
            buffer = jnp.where(living[:, None], buffer, jnp.zeros_like(buffer))
            buffer = feed_forward(buffer, norm_gain[section], up_weight[section], down_weight[section])
            planes.append(buffer)
        outputs.append(jnp.stack(planes))
        scores.append(found)
    return (jnp.stack(outputs, axis=1), jnp.stack(scores))
```

```python
import functools

import jax
import jax.numpy as jnp
from jax import lax
from jax.experimental import pallas as pl
from jax.experimental.pallas import tpu as pltpu
from jax.sharding import Mesh, PartitionSpec as P

EPSILON = 1e-05
SQRT_HALF = 0.7071067811865476
VMEM_LIMIT = 24 * 1024 * 1024
PLANE = ("dp", "y")
NT = (((1,), (1,)), ((), ()))


def normalise(own_ref, sib_ref, gain_ref, living, out_ref):
    blocks, half, cols = own_ref.shape
    width = blocks * cols
    for index, ref in enumerate((own_ref, sib_ref)):
        live = living[index * half : (index + 1) * half]

        def block(b, ref=ref, live=live):
            values = ref[b].astype(jnp.float32)
            return jnp.where(live, values, 0.0)

        total = jnp.zeros((half, cols), jnp.float32)
        for b in range(blocks):
            total += block(b)
        mean = jnp.sum(total, axis=1, keepdims=True) / width
        total = jnp.zeros((half, cols), jnp.float32)
        for b in range(blocks):
            center = block(b) - mean
            total += center * center
        scale = lax.rsqrt(jnp.sum(total, axis=1, keepdims=True) / width + EPSILON)
        for b in range(blocks):
            lanes = slice(b * cols, (b + 1) * cols)
            normed = (block(b) - mean) * scale * gain_ref[:, lanes]
            out_ref[index * half : (index + 1) * half, lanes] = normed.astype(jnp.bfloat16)


def section_kernel(
    section, last, own_ref, sib_ref, exit_ref, order_ref, gain_ref, up_ref, down_ref,
    keep_ref, send_ref, normed_ref
):
    blocks, half, cols = own_ref.shape
    rows = 2 * half
    rank = exit_ref[...]
    living = (rank == 0) | (rank > section)
    normalise(own_ref, sib_ref, gain_ref, living, normed_ref)
    pre = lax.dot_general(normed_ref[...], up_ref[...], NT, preferred_element_type=jnp.float32)
    hidden = (0.5 * pre * (1.0 + lax.erf(pre * SQRT_HALF))).astype(jnp.bfloat16)
    if last:
        slots = lax.broadcasted_iota(jnp.int32, (rows, rows), 1)
        choose = jnp.where(order_ref[...] == slots, 1.0, 0.0).astype(jnp.bfloat16)
        hidden = jnp.dot(choose, hidden, preferred_element_type=jnp.float32).astype(jnp.bfloat16)
    step = 2
    for b in range(0, blocks, step):
        part = jnp.dot(
            hidden, down_ref[:, b * cols : (b + step) * cols], preferred_element_type=jnp.float32
        ).astype(jnp.bfloat16)
        for k in range(step):
            keep_ref[b + k] = part[:half, k * cols : (k + 1) * cols]
            send_ref[b + k] = part[half:, k * cols : (k + 1) * cols]


def run_section(section, last, own, sib, ranks, order, gain, up_matrix, down_matrix):
    blocks, half, cols = own.shape
    vmem = pl.BlockSpec(memory_space=pltpu.VMEM)
    block = jax.ShapeDtypeStruct(own.shape, jnp.bfloat16)
    hidden = up_matrix.shape[0]
    return pl.pallas_call(
        functools.partial(section_kernel, section, last),
        out_shape=(block, block),
        in_specs=[vmem] * 7,
        out_specs=(vmem, vmem),
        scratch_shapes=[pltpu.VMEM((2 * half, blocks * cols), jnp.bfloat16)],
        compiler_params=pltpu.CompilerParams(vmem_limit_bytes=VMEM_LIMIT),
        cost_estimate=pl.CostEstimate(
            flops=8 * half * blocks * cols * hidden,
            bytes_accessed=4 * hidden * blocks * cols,
            transcendentals=2 * half * hidden,
        ),
        name="section",
    )(own, sib, ranks, order, gain, up_matrix, down_matrix)


def head_kernel(own_ref, sib_ref, wanted_ref, gain_ref, head_ref, out_ref, normed_ref):
    blocks, half, cols = own_ref.shape
    rows = 2 * half
    normalise(own_ref, sib_ref, gain_ref, jnp.full((rows, 1), True), normed_ref)
    logits = lax.dot_general(normed_ref[...], head_ref[...], NT, preferred_element_type=jnp.float32)
    exp_part = jnp.sum(jnp.exp(logits), axis=1, keepdims=True)
    columns = lax.broadcasted_iota(jnp.int32, logits.shape, 1)
    picked = jnp.sum(jnp.where(columns == wanted_ref[...], logits, 0.0), axis=1, keepdims=True)
    lane = lax.broadcasted_iota(jnp.int32, (rows, 128), 1)
    out_ref[...] = jnp.where(lane == 0, exp_part, jnp.where(lane == 1, picked, 0.0))


def run_head(own, sib, wanted, gain, head):
    blocks, half, cols = own.shape
    vmem = pl.BlockSpec(memory_space=pltpu.VMEM)
    return pl.pallas_call(
        head_kernel,
        out_shape=jax.ShapeDtypeStruct((2 * half, 128), jnp.float32),
        in_specs=[vmem] * 5,
        out_specs=vmem,
        scratch_shapes=[pltpu.VMEM((2 * half, blocks * cols), jnp.bfloat16)],
        compiler_params=pltpu.CompilerParams(vmem_limit_bytes=VMEM_LIMIT),
        cost_estimate=pl.CostEstimate(
            flops=4 * half * blocks * cols * head.shape[0],
            bytes_accessed=2 * head.shape[0] * blocks * cols,
            transcendentals=2 * half * head.shape[0],
        ),
        name="exit_head",
    )(own, sib, wanted, gain, head)


def swapped(value):
    return lax.ppermute(value, "core", [(0, 1), (1, 0)])


def exchanged(value):
    return lax.all_to_all(value, PLANE, 0, 0, tiled=True)


def on_device(inputs, exit_at, targets, repack, norm_gain, up_weight, down_weight, exit_gain, head):
    section_index = lax.axis_index("segment")
    section_count = lax.axis_size("segment")
    core = lax.axis_index("core")
    z_index = lax.axis_index("dp")
    y_index = lax.axis_index("y")
    blocks = lax.axis_size("dp")
    y_count = lax.axis_size("y")
    members = blocks * y_count
    width = inputs.shape[2]
    cols = width // blocks
    half = exit_at.shape[1] // 2
    sub = half // y_count
    place = z_index * y_count + y_index
    position = place * 2 + core
    group_index = position
    vocab_cols = head.shape[0]
    up_matrix, down_matrix = up_weight[0], down_weight[0]
    first, second_source = repack[0, 0], repack[0, 1]
    leaving = exit_at[0]

    def by_slot(values):
        pairs = values.reshape(half, 2)
        own = jnp.where(core == 0, pairs[:, 0], pairs[:, 1])
        sib = jnp.where(core == 0, pairs[:, 1], pairs[:, 0])
        return jnp.concatenate([own, sib])

    def slot_of(row):
        return row // 2 + half * (row % 2 != core).astype(jnp.int32)

    ranks = by_slot(leaving)[:, None]
    anchor_last = first[second_source]
    order = slot_of(by_slot(anchor_last))[:, None]
    wanted = by_slot(targets[0])[:, None] - group_index * vocab_cols
    own_anchor = jnp.where(
        section_index == 3,
        anchor_last[position],
        jnp.where(section_index == 2, first[position], position),
    )
    own_slot = slot_of(own_anchor)
    exit_scale = exit_gain[None, :]

    def row_of(own, sib):
        at = own_slot % half
        from_own = lax.dynamic_slice(own, (0, at, 0), (blocks, 1, cols))
        from_sib = lax.dynamic_slice(sib, (0, at, 0), (blocks, 1, cols))
        return jnp.where(own_slot < half, from_own, from_sib)[:, 0, :]

    def spread(chunk):
        return jnp.broadcast_to(chunk[None], (members, *chunk.shape))

    mine = inputs[0].reshape(blocks, cols)
    gathered = exchanged(spread(mine))
    own = jnp.swapaxes(gathered, 0, 1)
    chunk = lax.dynamic_slice(own, (z_index, y_index * sub, 0), (1, sub, cols))[0]
    kept = {}
    selected = jnp.zeros((blocks, cols), jnp.bfloat16)
    scores = None
    for section in range(4):
        last = section == 3
        if section:
            payload = spread(chunk)
            if last:

                def head_stats(own_in, sib_in):
                    stats = run_head(own_in, sib_in, wanted, exit_scale, head)[:, :2]
                    high = lax.reduce_precision(stats, 8, 7)
                    four = jnp.concatenate([high, stats - high], axis=1).astype(jnp.bfloat16)
                    four = jnp.stack([four[:half], four[half:]], axis=1)
                    return jnp.pad(four, ((0, 0), (0, sub - 2), (0, cols - 4)))

                payload = lax.switch(
                    section_index,
                    [
                        lambda: payload,
                        lambda: head_stats(*kept[1]),
                        lambda: head_stats(*kept[2]),
                        lambda: payload,
                    ],
                )
            own = exchanged(payload).reshape(blocks, half, cols)
        sib = swapped(own)
        if section:
            kept[section] = (own, sib)
            selected = jnp.where(section_index == section, row_of(own, sib), selected)
        if last:
            first_sums = own.reshape(members, sub, cols)[:, 0, :4].astype(jnp.float32)
            other_sums = sib.reshape(members, sub, cols)[:, 1, :4].astype(jnp.float32)
            sums = jnp.sum(first_sums + other_sums, axis=0)
            exp_total, picked = sums[0] + sums[2], sums[1] + sums[3]
            needs = (section_index >= 1) & (section_index <= 2)
            chosen = needs & (leaving[position] == section_index)
            score = jnp.where(chosen, picked - jnp.log(exp_total), 0.0)
            scores = lax.psum(score.reshape(1, 1), "segment")
        keep, send = run_section(
            section, last, own, sib, ranks, order, norm_gain, up_matrix, down_matrix
        )
        both = keep + swapped(send)
        if last:
            rank_here = leaving[own_anchor]
            living = (rank_here == 0) | (rank_here > section)
            summed = jnp.sum(exchanged(jnp.swapaxes(both, 0, 1)).astype(jnp.float32), axis=0)
            before = jnp.where(living, selected.astype(jnp.float32), 0.0)
            final = (before + summed).astype(jnp.bfloat16)
        else:
            rank_here = lax.dynamic_slice(ranks, (y_index * sub, 0), (sub, 1))
            living = (rank_here == 0) | (rank_here > section)
            parts = exchanged(both.reshape(members, sub, cols)).astype(jnp.float32)
            before = jnp.where(living, chunk.astype(jnp.float32), 0.0)
            result = (before + jnp.sum(parts, axis=0)).astype(jnp.bfloat16)
            chunk = lax.ppermute(
                result, "segment", [(i, i + 1) for i in range(section_count - 1)]
            )
    returned = lax.ppermute(selected, "segment", [(i + 1, i) for i in range(section_count - 1)])
    stored = jnp.where(section_index == section_count - 1, final, returned)
    return (stored.reshape(1, 1, 1, width), scores)


def solution(mesh):
    segments, groups, tensors = mesh.devices.shape
    fine = Mesh(
        mesh.devices.reshape(segments, groups, tensors // 2, 2), ("segment", "dp", "y", "core")
    )
    rows = ("dp", "y", "core")
    placed = (
        P(None, rows, None),
        P(),
        P(),
        P(),
        P("segment", None),
        P("segment", rows, None),
        P("segment", rows, None),
        P(),
        P(rows, None),
    )
    return jax.shard_map(
        on_device,
        mesh=fine,
        in_specs=placed,
        out_specs=(P("segment", None, rows, None), P(None, rows)),
        check_vma=False,
    )
```

```python
import functools

import jax
import jax.numpy as jnp
from jax import lax
from jax.experimental import pallas as pl
from jax.experimental.pallas import tpu as pltpu
from jax.sharding import Mesh, PartitionSpec as P

EPSILON = 1e-05
SQRT_HALF = 0.7071067811865476
VMEM_LIMIT = 16 * 1024 * 1024
SMALL_LIMIT = 4 * 1024 * 1024
PLANE = ("dp", "y")
NT = (((1,), (1,)), ((), ()))
VMEM = pl.BlockSpec(memory_space=pltpu.VMEM)
SMEM = pl.BlockSpec(memory_space=pltpu.SMEM)
ANY = pl.BlockSpec(memory_space=pl.ANY)
SMALL = pltpu.CompilerParams(vmem_limit_bytes=SMALL_LIMIT)


def prepare_kernel(
    exit_ref, target_ref, repack_ref, rank_ref, chunk_rank_ref, order_ref, wanted_ref, pick_ref, flag_ref
):
    half = rank_ref.shape[0]
    sub = chunk_rank_ref.shape[0]
    segment = lax.axis_index("segment")
    core = lax.axis_index("core")
    place = lax.axis_index("dp") * lax.axis_size("y") + lax.axis_index("y")
    first_row = lax.axis_index("y") * sub
    line = lax.broadcasted_iota(jnp.int32, (half, 1), 0)
    ranks = jnp.zeros((half, 1), jnp.int32)
    orders, wanteds = ranks, ranks
    for i in range(half):
        row = 2 * i + core
        anchor = repack_ref[0, 0, repack_ref[0, 1, row]]
        slot = anchor // 2 + jnp.where(anchor % 2 == core, 0, half)
        ranks = jnp.where(line == i, exit_ref[0, row], ranks)
        orders = jnp.where(line == i, slot, orders)
        wanteds = jnp.where(line == i, target_ref[0, row], wanteds)
    rank_ref[...] = ranks
    order_ref[...] = orders
    wanted_ref[...] = wanteds
    line = lax.broadcasted_iota(jnp.int32, (sub, 1), 0)
    ranks = jnp.zeros((sub, 1), jnp.int32)
    for i in range(sub):
        ranks = jnp.where(line == i, exit_ref[0, 2 * (first_row + i) + core], ranks)
    chunk_rank_ref[...] = ranks

    def anchor_of(position):
        first = repack_ref[0, 0, position]
        second = repack_ref[0, 0, repack_ref[0, 1, position]]
        return jnp.where(segment == 3, second, jnp.where(segment == 2, first, position))

    position = 2 * place + core
    mine = anchor_of(position)
    other = anchor_of(2 * place + 1 - core)
    lanes = lax.broadcasted_iota(jnp.int32, pick_ref.shape, 1)
    lines = lax.broadcasted_iota(jnp.int32, pick_ref.shape, 0)
    pick_ref[...] = (
        ((lines == 0) & (lanes == mine // 2)) | ((lines == 1) & (lanes == other // 2))
    ).astype(jnp.float32)
    chosen = (segment >= 1) & (segment <= 2) & (exit_ref[0, position] == segment)
    rank = exit_ref[0, mine]
    living = (rank == 0) | (rank > 3)
    lines = lax.broadcasted_iota(jnp.int32, flag_ref.shape, 0)
    flag_ref[...] = (
        ((lines == 0) & (mine % 2 == core)) | ((lines == 1) & chosen) | ((lines == 2) & living)
    ).astype(jnp.float32)


def prepare(exit_at, targets, repack, half, sub):
    column = jax.ShapeDtypeStruct((half, 1), jnp.int32)
    return pl.pallas_call(
        prepare_kernel,
        out_shape=(
            column,
            jax.ShapeDtypeStruct((sub, 1), jnp.int32),
            column,
            column,
            jax.ShapeDtypeStruct((8, half), jnp.float32),
            jax.ShapeDtypeStruct((8, 128), jnp.float32),
        ),
        in_specs=[SMEM] * 3,
        out_specs=(VMEM,) * 6,
        compiler_params=SMALL,
        name="prepare",
    )(exit_at, targets, repack)


def load_kernel(*refs):
    count = (len(refs) - 1) // 2
    sems = refs[-1]
    copies = [
        pltpu.make_async_copy(refs[i], refs[count + i], sems.at[i]) for i in range(count)
    ]
    for copy in copies:
        copy.start()
    for copy in copies:
        copy.wait()


def load(*arrays):
    return pl.pallas_call(
        load_kernel,
        out_shape=tuple(jax.ShapeDtypeStruct(a.shape, a.dtype) for a in arrays),
        in_specs=[ANY] * len(arrays),
        out_specs=(VMEM,) * len(arrays),
        scratch_shapes=[pltpu.SemaphoreType.DMA((len(arrays),))],
        compiler_params=SMALL,
        name="load",
    )(*arrays)


def normalise(rows_ref, gain_ref, living, out_ref):
    blocks, _, cols = rows_ref.shape
    width = blocks * cols

    def block(b):
        values = rows_ref[b].astype(jnp.float32)
        return values if living is None else jnp.where(living, values, 0.0)

    total = block(0)
    for b in range(1, blocks):
        total += block(b)
    mean = jnp.sum(total, axis=1, keepdims=True) / width
    total = jnp.zeros_like(total)
    for b in range(blocks):
        center = block(b) - mean
        total += center * center
    scale = lax.rsqrt(jnp.sum(total, axis=1, keepdims=True) / width + EPSILON)
    for b in range(blocks):
        lanes = slice(b * cols, (b + 1) * cols)
        normed = (block(b) - mean) * scale * gain_ref[:, lanes]
        out_ref[:, lanes] = normed.astype(jnp.bfloat16)


def hidden_of(normed, up_ref):
    pre = lax.dot_general(normed, up_ref[...], NT, preferred_element_type=jnp.float32)
    return (0.5 * pre * (1.0 + lax.erf(pre * SQRT_HALF))).astype(jnp.bfloat16)


def project(hidden_a, hidden_b, down_a_ref, down_b_ref, out_ref, step=2):
    blocks, _, cols = out_ref.shape
    for b in range(0, blocks, step):
        lanes = slice(b * cols, (b + step) * cols)
        part = jnp.dot(hidden_a, down_a_ref[:, lanes], preferred_element_type=jnp.float32)
        part += jnp.dot(hidden_b, down_b_ref[:, lanes], preferred_element_type=jnp.float32)
        part = part.astype(jnp.bfloat16)
        for k in range(step):
            out_ref[b + k] = part[:, k * cols : (k + 1) * cols]


def pick_rows(section, rows_ref, pick_ref, before_ref, picked_ref):
    here = lax.axis_index("segment") == section

    @pl.when(here)
    def _():
        pick = pick_ref[...].astype(jnp.bfloat16)
        for b in range(rows_ref.shape[0]):
            picked_ref[b] = jnp.dot(
                pick, rows_ref[b], preferred_element_type=jnp.float32
            ).astype(jnp.bfloat16)

    @pl.when(jnp.logical_not(here))
    def _():
        picked_ref[...] = before_ref[...]


def living_at(section, rank_ref):
    rank = rank_ref[...]
    return (rank == 0) | (rank > section)


def section_kernel(
    section, rows_ref, rank_ref, gain_ref, pick_ref, before_ref,
    up_a_ref, up_b_ref, down_a_ref, down_b_ref, out_ref, picked_ref, normed_ref
):
    normalise(rows_ref, gain_ref, living_at(section, rank_ref), normed_ref)
    normed = normed_ref[...]
    hidden_a = hidden_of(normed, up_a_ref)
    hidden_b = hidden_of(normed, up_b_ref)
    project(hidden_a, hidden_b, down_a_ref, down_b_ref, out_ref)
    pick_rows(section, rows_ref, pick_ref, before_ref, picked_ref)


def run_section(section, rows, ranks, gain, pick, before, weights):
    blocks, half, cols = rows.shape
    block = jax.ShapeDtypeStruct(rows.shape, jnp.bfloat16)
    hidden = 2 * weights[0].shape[0]
    return pl.pallas_call(
        functools.partial(section_kernel, section),
        out_shape=(block, jax.ShapeDtypeStruct(before.shape, jnp.bfloat16)),
        in_specs=[VMEM] * 9,
        out_specs=(VMEM, VMEM),
        scratch_shapes=[pltpu.VMEM((half, blocks * cols), jnp.bfloat16)],
        compiler_params=SMALL,
        cost_estimate=pl.CostEstimate(
            flops=4 * half * blocks * cols * hidden,
            bytes_accessed=4 * hidden * blocks * cols,
            transcendentals=half * hidden,
        ),
        name="section",
    )(rows, ranks, gain, pick, before, *weights)


def settle_kernel(section, parts_ref, chunk_ref, rank_ref, out_ref):
    total = jnp.where(living_at(section, rank_ref), chunk_ref[...].astype(jnp.float32), 0.0)
    summed = parts_ref[0].astype(jnp.float32)
    for k in range(1, parts_ref.shape[0]):
        summed += parts_ref[k].astype(jnp.float32)
    out_ref[...] = (total + summed).astype(jnp.bfloat16)


def settle(section, parts, chunk, chunk_ranks):
    return pl.pallas_call(
        functools.partial(settle_kernel, section),
        out_shape=jax.ShapeDtypeStruct(chunk.shape, jnp.bfloat16),
        in_specs=[VMEM] * 3,
        out_specs=VMEM,
        compiler_params=SMALL,
        name="settle",
    )(parts, chunk, chunk_ranks)


def spread_kernel(chunk_ref, out_ref):
    chunk = chunk_ref[...]
    for k in range(out_ref.shape[0]):
        out_ref[k] = chunk


def spread(members, chunk):
    return pl.pallas_call(
        spread_kernel,
        out_shape=jax.ShapeDtypeStruct((members, *chunk.shape), jnp.bfloat16),
        in_specs=[VMEM],
        out_specs=VMEM,
        compiler_params=SMALL,
        name="spread",
    )(chunk)


def last_up_kernel(
    section, rows_ref, rank_ref, gain_ref, pick_ref, before_ref, flag_ref,
    up_a_ref, up_b_ref, hidden_ref, picked_ref, score_ref, normed_ref
):
    blocks, half, _ = rows_ref.shape
    sub = half * blocks // (half * blocks // 8)
    normalise(rows_ref, gain_ref, living_at(section, rank_ref), normed_ref)
    normed = normed_ref[...]
    hidden_ref[0] = hidden_of(normed, up_a_ref)
    hidden_ref[1] = hidden_of(normed, up_b_ref)
    pick_rows(section, rows_ref, pick_ref, before_ref, picked_ref)
    sums = jnp.zeros((sub, 128), jnp.float32)
    for b in range(blocks):
        for r in range(0, half, sub):
            sums += rows_ref[b, r : r + sub, :128].astype(jnp.float32)
    exp_total = sums[0:1, 0:1] + sums[0:1, 2:3]
    picked = sums[0:1, 1:2] + sums[0:1, 3:4]
    score = jnp.where(flag_ref[1:2, 0:1] > 0.0, picked - jnp.log(exp_total), 0.0)
    score_ref[...] = jnp.broadcast_to(score, score_ref.shape)


def run_last_up(section, rows, ranks, gain, pick, before, flags, up_a, up_b):
    blocks, half, cols = rows.shape
    hidden = up_a.shape[0]
    return pl.pallas_call(
        functools.partial(last_up_kernel, section),
        out_shape=(
            jax.ShapeDtypeStruct((2, half, hidden), jnp.bfloat16),
            jax.ShapeDtypeStruct(before.shape, jnp.bfloat16),
            jax.ShapeDtypeStruct((8, 128), jnp.float32),
        ),
        in_specs=[VMEM] * 8,
        out_specs=(VMEM,) * 3,
        scratch_shapes=[pltpu.VMEM((half, blocks * cols), jnp.bfloat16)],
        compiler_params=SMALL,
        cost_estimate=pl.CostEstimate(
            flops=4 * half * blocks * cols * hidden,
            bytes_accessed=4 * hidden * blocks * cols,
            transcendentals=2 * half * hidden,
        ),
        name="last_up",
    )(rows, ranks, gain, pick, before, flags, up_a, up_b)


def last_down_kernel(own_ref, sib_ref, order_ref, down_a_ref, down_b_ref, out_ref):
    half = own_ref.shape[1]
    slots = lax.broadcasted_iota(jnp.int32, (half, half), 1)
    order = order_ref[...]
    from_own = jnp.where(order == slots, 1.0, 0.0).astype(jnp.bfloat16)
    from_sib = jnp.where(order == slots + half, 1.0, 0.0).astype(jnp.bfloat16)

    def chosen(own, sib):
        rows = jnp.dot(from_own, own, preferred_element_type=jnp.float32)
        rows += jnp.dot(from_sib, sib, preferred_element_type=jnp.float32)
        return rows.astype(jnp.bfloat16)

    hidden_a = chosen(own_ref[0], sib_ref[1])
    hidden_b = chosen(own_ref[1], sib_ref[0])
    project(hidden_a, hidden_b, down_a_ref, down_b_ref, out_ref)


def run_last_down(shape, own, sib, order, down_a, down_b):
    blocks, half, cols = shape
    hidden = down_a.shape[0]
    return pl.pallas_call(
        last_down_kernel,
        out_shape=jax.ShapeDtypeStruct(shape, jnp.bfloat16),
        in_specs=[VMEM] * 5,
        out_specs=VMEM,
        compiler_params=SMALL,
        cost_estimate=pl.CostEstimate(
            flops=4 * half * blocks * cols * hidden,
            bytes_accessed=4 * hidden * blocks * cols,
            transcendentals=0,
        ),
        name="last_down",
    )(own, sib, order, down_a, down_b)


def payload_kernel(
    chunk_ref, first_ref, second_ref, wanted_ref, gain_ref, head_a_ref, head_b_ref, out_ref,
    rows_ref, normed_ref, a_ref, b_ref, sems
):
    members = out_ref.shape[0]
    segment = lax.axis_index("segment")
    core = lax.axis_index("core")
    place = lax.axis_index("dp") * lax.axis_size("y") + lax.axis_index("y")
    scoring = (segment >= 1) & (segment <= 2)

    @pl.when(jnp.logical_not(scoring))
    def _():
        chunk = chunk_ref[...]
        for k in range(members):
            out_ref[k] = chunk

    @pl.when(scoring)
    def _():
        copy_a = pltpu.make_async_copy(head_a_ref, a_ref, sems.at[0])
        copy_b = pltpu.make_async_copy(head_b_ref, b_ref, sems.at[1])
        copy_a.start()
        copy_b.start()

        @pl.when(segment == 1)
        def _():
            copy = pltpu.make_async_copy(first_ref, rows_ref, sems.at[2])
            copy.start()
            copy.wait()

        @pl.when(segment == 2)
        def _():
            copy = pltpu.make_async_copy(second_ref, rows_ref, sems.at[2])
            copy.start()
            copy.wait()

        normalise(rows_ref, gain_ref, None, normed_ref)
        normed = normed_ref[...]
        half, vocab = normed.shape[0], a_ref.shape[0]
        wanted = wanted_ref[...]
        exp_part = jnp.zeros((half, 1), jnp.float32)
        picked = jnp.zeros((half, 1), jnp.float32)
        for copy, ref, shard in (
            (copy_a, a_ref, 2 * place + core),
            (copy_b, b_ref, 2 * place + 1 - core),
        ):
            copy.wait()
            logits = lax.dot_general(normed, ref[...], NT, preferred_element_type=jnp.float32)
            exp_part += jnp.sum(jnp.exp(logits), axis=1, keepdims=True)
            columns = lax.broadcasted_iota(jnp.int32, logits.shape, 1) + shard * vocab
            picked += jnp.sum(jnp.where(columns == wanted, logits, 0.0), axis=1, keepdims=True)
        lane = lax.broadcasted_iota(jnp.int32, (half, 128), 1)
        both = jnp.where(lane % 2 == 0, exp_part, picked)
        high = both.astype(jnp.bfloat16).astype(jnp.float32)
        stats = jnp.where(lane < 2, high, jnp.where(lane < 4, both - high, 0.0))
        out_ref[...] = jnp.zeros_like(out_ref)
        top = lax.broadcasted_iota(jnp.int32, (out_ref.shape[1], 128), 0) == 0
        for k in range(members):
            out_ref[k, :, :128] = jnp.where(top, stats[k : k + 1], 0.0).astype(jnp.bfloat16)


def run_payload(members, chunk, first, second, wanted, gain, head_a, head_b):
    blocks, half, cols = first.shape
    return pl.pallas_call(
        payload_kernel,
        out_shape=jax.ShapeDtypeStruct((members, *chunk.shape), jnp.bfloat16),
        in_specs=[VMEM, ANY, ANY, VMEM, VMEM, ANY, ANY],
        out_specs=VMEM,
        scratch_shapes=[
            pltpu.VMEM(first.shape, jnp.bfloat16),
            pltpu.VMEM((half, blocks * cols), jnp.bfloat16),
            pltpu.VMEM(head_a.shape, jnp.bfloat16),
            pltpu.VMEM(head_b.shape, jnp.bfloat16),
            pltpu.SemaphoreType.DMA((3,)),
        ],
        compiler_params=pltpu.CompilerParams(vmem_limit_bytes=VMEM_LIMIT),
        name="payload",
    )(chunk, first, second, wanted, gain, head_a, head_b)


def swapped(value):
    return lax.ppermute(value, "core", [(0, 1), (1, 0)])


def exchanged(value):
    return lax.all_to_all(value, PLANE, 0, 0, tiled=True)


def on_device(inputs, exit_at, targets, repack, norm_gain, up_weight, down_weight, exit_gain, head):
    section_index = lax.axis_index("segment")
    section_count = lax.axis_size("segment")
    z_index = lax.axis_index("dp")
    y_index = lax.axis_index("y")
    blocks = lax.axis_size("dp")
    y_count = lax.axis_size("y")
    members = blocks * y_count
    width = inputs.shape[2]
    cols = width // blocks
    half = exit_at.shape[1] // 2
    sub = half // y_count
    up_a, down_a = up_weight[0], down_weight[0]
    up_b, down_b = swapped(up_a), swapped(down_a)

    def hop(value, step):
        pairs = [(i, (i + step) % section_count) for i in range(section_count)]
        return lax.ppermute(value, "segment", pairs)

    mine = inputs[0].reshape(blocks, cols)
    rows = jnp.swapaxes(exchanged(spread(members, mine)), 0, 1)
    ranks, chunk_ranks, order, wanted, pick, flags = prepare(exit_at, targets, repack, half, sub)
    chunk = lax.dynamic_slice(rows, (z_index, y_index * sub, 0), (1, sub, cols))[0]
    rows, chunk, up_a, up_b, down_a, down_b = lax.optimization_barrier(
        (rows, chunk, up_a, up_b, down_a, down_b)
    )
    up_a, up_b, down_a, down_b = load(up_a, up_b, down_a, down_b)
    weights = (up_a, up_b, down_a, down_b)
    picked = jnp.zeros((blocks, 8, cols), jnp.bfloat16)
    kept = []
    for section in range(3):
        if section:
            rows = exchanged(spread(members, chunk)).reshape(blocks, half, cols)
            kept.append(rows)
        parts, picked = run_section(section, rows, ranks, norm_gain, pick, picked, weights)
        parts = exchanged(parts.reshape(members, sub, cols))
        chunk = hop(settle(section, parts, chunk, chunk_ranks), 1)
    head_sib = swapped(head)
    payload = run_payload(members, chunk, *kept, wanted, exit_gain[None, :], head, head_sib)
    rows = exchanged(payload).reshape(blocks, half, cols)
    hidden, picked, score = run_last_up(
        3, rows, ranks, norm_gain, pick, picked, flags, up_a, up_b
    )
    parts = run_last_down(rows.shape, hidden, swapped(hidden), order, down_a, down_b)
    parts = exchanged(jnp.swapaxes(parts, 0, 1)).astype(jnp.float32)
    score = score[:1, :1]
    scores = score + hop(score, 1) + hop(score, 2) + hop(score, 3)
    selected = jnp.where(flags[0:1, 0:1] > 0, picked[:, 0], swapped(picked[:, 1]))
    returned = hop(selected, -1)
    before = jnp.where(flags[2:3, 0:1] > 0, selected.astype(jnp.float32), 0.0)
    final = (before + jnp.sum(parts, axis=0)).astype(jnp.bfloat16)
    stored = jnp.where(section_index == section_count - 1, final, returned)
    return (stored.reshape(1, 1, 1, width), scores)


def solution(mesh):
    segments, groups, tensors = mesh.devices.shape
    fine = Mesh(
        mesh.devices.reshape(segments, groups, tensors // 2, 2), ("segment", "dp", "y", "core")
    )
    rows = ("dp", "y", "core")
    placed = (
        P(None, rows, None),
        P(),
        P(),
        P(),
        P("segment", None),
        P("segment", rows, None),
        P("segment", rows, None),
        P(),
        P(rows, None),
    )
    return jax.shard_map(
        on_device,
        mesh=fine,
        in_specs=placed,
        out_specs=(P("segment", None, rows, None), P(None, rows)),
        check_vma=False,
    )
```

```python
import functools

import jax
import jax.numpy as jnp
from jax import lax
from jax.experimental import pallas as pl
from jax.experimental.pallas import tpu as pltpu
from jax.sharding import Mesh, PartitionSpec as P

EPSILON = 1e-05
SQRT_HALF = 0.7071067811865476
PAYLOAD_LIMIT = 12 * 1024 * 1024
FIRST_LIMIT = 39 * 1024 * 1024
SMALL_LIMIT = 4 * 1024 * 1024
PLANE = ("dp", "y")
NT = (((1,), (1,)), ((), ()))
VMEM = pl.BlockSpec(memory_space=pltpu.VMEM)
SMEM = pl.BlockSpec(memory_space=pltpu.SMEM)
HBM = pl.BlockSpec(memory_space=pltpu.HBM)
SMALL = pltpu.CompilerParams(vmem_limit_bytes=SMALL_LIMIT)


def row_at(repack_ref, position):
    return repack_ref[0, 0, repack_ref[0, 1, position]]


def prepare_kernel(
    exit_ref, target_ref, repack_ref, gain_ref, rank_ref, chunk_rank_ref, wanted_ref, pick_ref,
    source_ref, flag_ref, ready_gain_ref
):
    half = rank_ref.shape[0]
    sub = chunk_rank_ref.shape[0]
    segment = lax.axis_index("segment")
    core = lax.axis_index("core")
    place = lax.axis_index("dp") * lax.axis_size("y") + lax.axis_index("y")
    first_row = lax.axis_index("y") * sub

    def source_of(position):
        first = repack_ref[0, 0, position]
        last = row_at(repack_ref, position)
        return jnp.where(segment == 3, last, jnp.where(segment == 2, first, position))

    mine = source_of(2 * place + core)
    other = source_of(2 * place + 1 - core)
    line = lax.broadcasted_iota(jnp.int32, (half, 1), 0)
    pick_line = lax.broadcasted_iota(jnp.int32, pick_ref.shape, 0)
    pick_lane = lax.broadcasted_iota(jnp.int32, pick_ref.shape, 1)
    ranks = jnp.zeros((half, 1), jnp.int32)
    wanteds = ranks
    sources = jnp.zeros(pick_ref.shape, jnp.int32)
    here, there = 0, 0
    for i in range(half):
        row = row_at(repack_ref, 2 * i + core)
        ranks = jnp.where(line == i, exit_ref[0, row], ranks)
        wanteds = jnp.where(line == i, target_ref[0, row], wanteds)
        sources = jnp.where(pick_lane == i, row, sources)
        here = jnp.where(row == 2 * place + core, 1, here)
        there = jnp.where(row == 2 * place + 1 - core, 1, there)
    rank_ref[...] = ranks
    wanted_ref[...] = wanteds
    source_ref[...] = sources
    ready_gain_ref[...] = gain_ref[...]
    pick_ref[...] = (
        ((pick_line == 0) & (sources == mine)) | ((pick_line == 1) & (sources == other))
    ).astype(jnp.float32)
    line = lax.broadcasted_iota(jnp.int32, (sub, 1), 0)
    ranks = jnp.zeros((sub, 1), jnp.int32)
    for i in range(sub):
        row = row_at(repack_ref, 2 * (first_row + i) + core)
        ranks = jnp.where(line == i, exit_ref[0, row], ranks)
    chunk_rank_ref[...] = ranks
    scoring = (segment >= 1) & (segment <= 2)
    chosen = scoring & (here == 1) & (exit_ref[0, 2 * place + core] == segment)
    other_chosen = scoring & (there == 1) & (exit_ref[0, 2 * place + 1 - core] == segment)
    rank = exit_ref[0, row_at(repack_ref, 2 * place + core)]
    living = (rank == 0) | (rank > 3)
    lines = lax.broadcasted_iota(jnp.int32, flag_ref.shape, 0)
    flag_ref[...] = (
        ((lines == 0) & chosen) | ((lines == 1) & other_chosen) | ((lines == 2) & living)
    ).astype(jnp.float32)


def prepare(exit_at, targets, repack, gain, half, sub):
    column = jax.ShapeDtypeStruct((half, 1), jnp.int32)
    return pl.pallas_call(
        prepare_kernel,
        out_shape=(
            column,
            jax.ShapeDtypeStruct((sub, 1), jnp.int32),
            column,
            jax.ShapeDtypeStruct((8, half), jnp.float32),
            jax.ShapeDtypeStruct((8, half), jnp.int32),
            jax.ShapeDtypeStruct((8, 128), jnp.float32),
            jax.ShapeDtypeStruct(gain.shape, gain.dtype),
        ),
        in_specs=[SMEM] * 3 + [VMEM],
        out_specs=(VMEM,) * 7,
        compiler_params=SMALL,
        name="prepare",
    )(exit_at, targets, repack, gain)


def normalise(rows_ref, gain_ref, living, out_ref):
    blocks, _, cols = rows_ref.shape
    width = blocks * cols
    total = rows_ref[0].astype(jnp.float32)
    for b in range(1, blocks):
        total += rows_ref[b].astype(jnp.float32)
    mean = jnp.sum(total, axis=1, keepdims=True) / width
    total = jnp.zeros_like(total)
    for b in range(blocks):
        lanes = slice(b * cols, (b + 1) * cols)
        center = rows_ref[b].astype(jnp.float32) - mean
        total += center * center
        out_ref[:, lanes] = (center * gain_ref[:, lanes]).astype(jnp.bfloat16)
    scale = lax.rsqrt(jnp.sum(total, axis=1, keepdims=True) / width + EPSILON)
    return scale if living is None else jnp.where(living, scale, 0.0)


def hidden_of(normed, scale, up_ref):
    pre = lax.dot_general(normed, up_ref[...], NT, preferred_element_type=jnp.float32) * scale
    return (0.5 * pre * (1.0 + lax.erf(pre * SQRT_HALF))).astype(jnp.bfloat16)


def project(hidden_a, hidden_b, down_a_ref, down_b_ref, out_ref, step=2):
    blocks, _, cols = out_ref.shape
    for b in range(0, blocks, step):
        lanes = slice(b * cols, (b + step) * cols)
        part = jnp.dot(hidden_a, down_a_ref[:, lanes], preferred_element_type=jnp.float32)
        part += jnp.dot(hidden_b, down_b_ref[:, lanes], preferred_element_type=jnp.float32)
        part = part.astype(jnp.bfloat16)
        for k in range(step):
            out_ref[b + k] = part[:, k * cols : (k + 1) * cols]


def pick_rows(section, rows_ref, pick_ref, before_ref, picked_ref):
    here = lax.axis_index("segment") == section

    def choose():
        pick = pick_ref[...].astype(jnp.bfloat16)
        for b in range(rows_ref.shape[0]):
            picked_ref[b] = jnp.dot(
                pick, rows_ref[b], preferred_element_type=jnp.float32
            ).astype(jnp.bfloat16)

    def keep():
        picked_ref[...] = before_ref[...]

    if before_ref is None:
        choose()
    else:
        pl.when(here)(choose)
        pl.when(jnp.logical_not(here))(keep)


def living_at(section, rank_ref):
    rank = rank_ref[...]
    return (rank == 0) | (rank > section)


def section_kernel(section, rows_ref, rank_ref, gain_ref, pick_ref, *refs):
    before_ref = refs[0] if len(refs) == 8 else None
    up_a_ref, up_b_ref, down_a_ref, down_b_ref, out_ref, picked_ref, normed_ref = refs[-7:]
    scale = normalise(rows_ref, gain_ref, living_at(section, rank_ref), normed_ref)
    normed = normed_ref[...]
    hidden_a = hidden_of(normed, scale, up_a_ref)
    hidden_b = hidden_of(normed, scale, up_b_ref)
    project(hidden_a, hidden_b, down_a_ref, down_b_ref, out_ref)
    pick_rows(section, rows_ref, pick_ref, before_ref, picked_ref)


def run_section(section, rows, ranks, gain, pick, before, weights):
    blocks, half, cols = rows.shape
    block = jax.ShapeDtypeStruct(rows.shape, jnp.bfloat16)
    hidden = 2 * weights[0].shape[0]
    return pl.pallas_call(
        functools.partial(section_kernel, section),
        out_shape=(block, jax.ShapeDtypeStruct((blocks, pick.shape[0], cols), jnp.bfloat16)),
        in_specs=[VMEM] * (8 + len(before)),
        out_specs=(VMEM, VMEM),
        scratch_shapes=[pltpu.VMEM((half, blocks * cols), jnp.bfloat16)],
        compiler_params=SMALL,
        cost_estimate=pl.CostEstimate(
            flops=4 * half * blocks * cols * hidden,
            bytes_accessed=4 * hidden * blocks * cols,
            transcendentals=half * hidden,
        ),
        name="section",
    )(rows, ranks, gain, pick, *before, *weights)


def settle_kernel(section, parts_ref, chunk_ref, rank_ref, out_ref):
    total = jnp.where(living_at(section, rank_ref), chunk_ref[...].astype(jnp.float32), 0.0)
    summed = parts_ref[0].astype(jnp.float32)
    for k in range(1, parts_ref.shape[0]):
        summed += parts_ref[k].astype(jnp.float32)
    out_ref[...] = (total + summed).astype(jnp.bfloat16)


def settle(section, parts, chunk, chunk_ranks):
    return pl.pallas_call(
        functools.partial(settle_kernel, section),
        out_shape=jax.ShapeDtypeStruct(chunk.shape, jnp.bfloat16),
        in_specs=[VMEM] * 3,
        out_specs=VMEM,
        compiler_params=SMALL,
        name="settle",
    )(parts, chunk, chunk_ranks)


def spread_kernel(chunk_ref, out_ref):
    chunk = chunk_ref[...]
    for k in range(out_ref.shape[0]):
        out_ref[k] = chunk


def spread(members, chunk):
    return pl.pallas_call(
        spread_kernel,
        out_shape=jax.ShapeDtypeStruct((members, *chunk.shape), jnp.bfloat16),
        in_specs=[VMEM],
        out_specs=VMEM,
        compiler_params=SMALL,
        name="spread",
    )(chunk)


def first_spread_kernel(row_ref, out_ref):
    members, blocks, cols = out_ref.shape
    row = row_ref[0].astype(jnp.float32)
    line = lax.broadcasted_iota(jnp.int32, (blocks, cols), 0)
    chunk = jnp.zeros((blocks, cols), jnp.float32)
    for b in range(blocks):
        chunk = jnp.where(line == b, row[:, b * cols : (b + 1) * cols], chunk)
    chunk = chunk.astype(jnp.bfloat16)
    for k in range(members):
        out_ref[k] = chunk


def first_spread(members, blocks, row):
    return pl.pallas_call(
        first_spread_kernel,
        out_shape=jax.ShapeDtypeStruct((members, blocks, row.shape[-1] // blocks), row.dtype),
        in_specs=[VMEM],
        out_specs=VMEM,
        compiler_params=SMALL,
        name="first_spread",
    )(row)


def first_section_kernel(own_ref, sib_ref, repack_ref, gain_ref, *refs):
    held_refs, (out_ref, chunk_ref), ready_refs = refs[:4], refs[4:6], refs[6:10]
    gathered_ref, rows_ref, normed_ref, sems = refs[10:]
    copies = [
        pltpu.make_async_copy(held, ready, sems.at[i])
        for i, (held, ready) in enumerate(zip(held_refs, ready_refs))
    ]
    copies[0].start()
    copies[1].start()
    members, blocks, cols = gathered_ref.shape
    sub = chunk_ref.shape[0]
    core = lax.axis_index("core")
    for i in range(members):
        row = row_at(repack_ref, 2 * i + core)
        gathered_ref[i] = jnp.where(row % 2 == core, own_ref[row // 2], sib_ref[row // 2])
    copies[2].start()
    copies[3].start()
    rows = jnp.swapaxes(gathered_ref[...].astype(jnp.float32), 0, 1)
    rows_ref[...] = rows.astype(jnp.bfloat16)
    scale = normalise(rows_ref, gain_ref, None, normed_ref)
    block = lax.axis_index("dp")
    first_row = lax.axis_index("y") * sub
    line = lax.broadcasted_iota(jnp.int32, (blocks, cols), 0)
    chunk = jnp.zeros((sub, cols), jnp.float32)
    for r in range(sub):
        tile = gathered_ref[first_row + r].astype(jnp.float32)
        row = jnp.sum(jnp.where(line == block, tile, 0.0), axis=0, keepdims=True)
        chunk = jnp.where(line[:sub] == r, row, chunk)
    chunk_ref[...] = chunk.astype(jnp.bfloat16)
    up_a_ref, up_b_ref, down_a_ref, down_b_ref = ready_refs
    normed = normed_ref[...]
    copies[0].wait()
    hidden_a = hidden_of(normed, scale, up_a_ref)
    copies[1].wait()
    hidden_b = hidden_of(normed, scale, up_b_ref)
    copies[2].wait()
    copies[3].wait()
    project(hidden_a, hidden_b, down_a_ref, down_b_ref, out_ref)


def run_first_section(own, sib, repack, gain, sub, weights):
    members, blocks, cols = own.shape
    shape = (blocks, members, cols)
    hidden = 2 * weights[0].shape[0]
    return pl.pallas_call(
        first_section_kernel,
        out_shape=(
            jax.ShapeDtypeStruct(shape, jnp.bfloat16),
            jax.ShapeDtypeStruct((sub, cols), jnp.bfloat16),
            *(jax.ShapeDtypeStruct(w.shape, w.dtype) for w in weights),
        ),
        in_specs=[VMEM, VMEM, SMEM, VMEM] + [HBM] * 4,
        out_specs=(VMEM,) * 6,
        scratch_shapes=[
            pltpu.VMEM(own.shape, jnp.bfloat16),
            pltpu.VMEM(shape, jnp.bfloat16),
            pltpu.VMEM((members, blocks * cols), jnp.bfloat16),
            pltpu.SemaphoreType.DMA((4,)),
        ],
        compiler_params=pltpu.CompilerParams(vmem_limit_bytes=FIRST_LIMIT),
        cost_estimate=pl.CostEstimate(
            flops=4 * members * blocks * cols * hidden,
            bytes_accessed=4 * hidden * blocks * cols,
            transcendentals=members * hidden,
        ),
        name="first_section",
    )(own, sib, repack, gain, *weights)


def last_section_kernel(
    section, rows_ref, rank_ref, gain_ref, pick_ref, before_ref, flag_ref,
    up_a_ref, up_b_ref, down_a_ref, down_b_ref,
    out_ref, mine_ref, other_ref, score_ref, other_score_ref, normed_ref, picked_ref, parts_ref
):
    blocks, half, cols = rows_ref.shape
    core = lax.axis_index("core")

    @pl.when(lax.axis_index("segment") == section)
    def _():
        section_kernel(
            section, rows_ref, rank_ref, gain_ref, pick_ref, None,
            up_a_ref, up_b_ref, down_a_ref, down_b_ref, parts_ref, picked_ref, normed_ref
        )
        parts = jnp.swapaxes(parts_ref[...].astype(jnp.float32), 0, 1)
        out_ref[...] = parts.astype(jnp.bfloat16)

    @pl.when(lax.axis_index("segment") != section)
    def _():
        picked_ref[...] = before_ref[...]

    line = lax.broadcasted_iota(jnp.int32, (blocks, cols), 0)
    mine = jnp.zeros((blocks, cols), jnp.float32)
    other = mine
    for b in range(blocks):
        tile = picked_ref[b].astype(jnp.float32)
        mine = jnp.where(line == b, tile[0:1], mine)
        other = jnp.where(line == b, tile[1:2], other)
    mine_ref[...] = mine.astype(jnp.bfloat16)
    other_ref[...] = other.astype(jnp.bfloat16)
    sub = flag_ref.shape[0]
    sums = jnp.zeros(flag_ref.shape, jnp.float32)
    for b in range(blocks):
        for r in range(0, half, sub):
            sums += rows_ref[b, r : r + sub, :128].astype(jnp.float32)
    for index, ref in enumerate((score_ref, other_score_ref)):
        stats = jnp.where(core == index, sums[0:1], sums[1:2])
        exp_total = stats[:, 0:1] + stats[:, 2:3]
        picked = stats[:, 1:2] + stats[:, 3:4]
        flag = flag_ref[index : index + 1, 0:1]
        score = jnp.where(flag > 0.0, picked - jnp.log(exp_total), 0.0)
        ref[...] = jnp.broadcast_to(score, ref.shape)


def run_last_section(section, rows, ranks, gain, pick, before, flags, weights):
    blocks, half, cols = rows.shape
    hidden = 2 * weights[0].shape[0]
    row = jax.ShapeDtypeStruct((blocks, cols), jnp.bfloat16)
    score = jax.ShapeDtypeStruct((1, 128), jnp.float32)
    return pl.pallas_call(
        functools.partial(last_section_kernel, section),
        out_shape=(
            jax.ShapeDtypeStruct((half, blocks, cols), jnp.bfloat16), row, row, score, score
        ),
        in_specs=[VMEM] * 10,
        out_specs=(VMEM,) * 5,
        scratch_shapes=[
            pltpu.VMEM((half, blocks * cols), jnp.bfloat16),
            pltpu.VMEM(before.shape, jnp.bfloat16),
            pltpu.VMEM(rows.shape, jnp.bfloat16),
        ],
        compiler_params=SMALL,
        cost_estimate=pl.CostEstimate(
            flops=4 * half * blocks * cols * hidden,
            bytes_accessed=4 * hidden * blocks * cols,
            transcendentals=half * hidden,
        ),
        name="last_section",
    )(rows, ranks, gain, pick, before, flags, *weights)


def finish_kernel(section, parts_ref, row_ref, returned_ref, flag_ref, out_ref):
    blocks, cols = row_ref.shape
    here = lax.axis_index("segment") == section

    @pl.when(here)
    def _():
        total = jnp.where(flag_ref[2:3, 0:1] > 0.0, row_ref[...].astype(jnp.float32), 0.0)
        summed = parts_ref[0].astype(jnp.float32)
        for k in range(1, parts_ref.shape[0]):
            summed += parts_ref[k].astype(jnp.float32)
        total += summed
        for b in range(blocks):
            out_ref[0, 0, :, b * cols : (b + 1) * cols] = total[b : b + 1].astype(jnp.bfloat16)

    @pl.when(jnp.logical_not(here))
    def _():
        total = returned_ref[...].astype(jnp.float32)
        for b in range(blocks):
            out_ref[0, 0, :, b * cols : (b + 1) * cols] = total[b : b + 1].astype(jnp.bfloat16)


def finish(section, parts, row, returned, flags):
    width = row.shape[0] * row.shape[1]
    return pl.pallas_call(
        functools.partial(finish_kernel, section),
        out_shape=jax.ShapeDtypeStruct((1, 1, 1, width), jnp.bfloat16),
        in_specs=[VMEM] * 4,
        out_specs=VMEM,
        compiler_params=SMALL,
        name="finish",
    )(parts, row, returned, flags)


def payload_kernel(
    chunk_ref, first_ref, second_ref, source_ref, wanted_ref, gain_ref, head_a_ref, head_b_ref,
    out_ref, rows_ref, normed_ref, held_ref, sem
):
    members = out_ref.shape[0]
    segment = lax.axis_index("segment")
    core = lax.axis_index("core")
    place = lax.axis_index("dp") * lax.axis_size("y") + lax.axis_index("y")
    scoring = (segment >= 1) & (segment <= 2)

    @pl.when(jnp.logical_not(scoring))
    def _():
        chunk = chunk_ref[...]
        for k in range(members):
            out_ref[k] = chunk

    @pl.when(segment == 1)
    def _():
        rows_ref[...] = first_ref[...]

    @pl.when(segment == 2)
    def _():
        rows_ref[...] = second_ref[...]

    @pl.when(scoring)
    def _():
        copy = pltpu.make_async_copy(head_b_ref, held_ref, sem)
        copy.start()
        scale = normalise(rows_ref, gain_ref, None, normed_ref)
        normed = normed_ref[...]
        half, vocab = normed.shape[0], head_a_ref.shape[0]
        wanted = wanted_ref[...]
        exp_part = jnp.zeros((half, 1), jnp.float32)
        picked = jnp.zeros((half, 1), jnp.float32)
        for ref, shard in (
            (head_a_ref, 2 * place + core),
            (held_ref, 2 * place + 1 - core),
        ):
            if ref is held_ref:
                copy.wait()
            logits = lax.dot_general(normed, ref[...], NT, preferred_element_type=jnp.float32)
            logits *= scale
            exp_part += jnp.sum(jnp.exp(logits), axis=1, keepdims=True)
            columns = lax.broadcasted_iota(jnp.int32, logits.shape, 1) + shard * vocab
            picked += jnp.sum(jnp.where(columns == wanted, logits, 0.0), axis=1, keepdims=True)
        lane = lax.broadcasted_iota(jnp.int32, (half, 128), 1)
        both = jnp.where(lane % 2 == 0, exp_part, picked)
        high = both.astype(jnp.bfloat16).astype(jnp.float32)
        stats = jnp.where(lane < 2, high, jnp.where(lane < 4, both - high, 0.0))
        out_ref[...] = jnp.zeros_like(out_ref)
        stats = stats.astype(jnp.bfloat16)
        target = 2 * lax.broadcasted_iota(jnp.int32, (members, half), 0)
        sorted_stats = [
            jnp.dot(
                jnp.where(source_ref[0:1, :] == target + parity, 1.0, 0.0).astype(jnp.bfloat16),
                stats,
                preferred_element_type=jnp.float32,
            )
            for parity in range(2)
        ]
        line = lax.broadcasted_iota(jnp.int32, (out_ref.shape[1], 128), 0)
        for k in range(members):
            even, odd = (part[k : k + 1] for part in sorted_stats)
            tile = jnp.where(line == 0, even, jnp.where(line == 1, odd, 0.0))
            out_ref[k, :, :128] = tile.astype(jnp.bfloat16)


def run_payload(members, chunk, first, second, sources, wanted, gain, head_a, head_b):
    blocks, half, cols = first.shape
    return pl.pallas_call(
        payload_kernel,
        out_shape=jax.ShapeDtypeStruct((members, *chunk.shape), jnp.bfloat16),
        in_specs=[VMEM] * 7 + [HBM],
        out_specs=VMEM,
        scratch_shapes=[
            pltpu.VMEM(first.shape, jnp.bfloat16),
            pltpu.VMEM((half, blocks * cols), jnp.bfloat16),
            pltpu.VMEM(head_b.shape, jnp.bfloat16),
            pltpu.SemaphoreType.DMA,
        ],
        compiler_params=pltpu.CompilerParams(vmem_limit_bytes=PAYLOAD_LIMIT),
        name="payload",
    )(chunk, first, second, sources, wanted, gain, head_a, head_b)


def swapped(value):
    return lax.ppermute(value, "core", [(0, 1), (1, 0)])


def exchanged(value):
    return lax.all_to_all(value, PLANE, 0, 0, tiled=True)


def on_device(inputs, exit_at, targets, repack, norm_gain, up_weight, down_weight, exit_gain, head):
    section_count = lax.axis_size("segment")
    blocks = lax.axis_size("dp")
    y_count = lax.axis_size("y")
    members = blocks * y_count
    cols = inputs.shape[2] // blocks
    half = exit_at.shape[1] // 2
    sub = half // y_count
    up_a, down_a = up_weight[0], down_weight[0]
    up_b, down_b = swapped(up_a), swapped(down_a)

    def hop(value, step):
        pairs = [(i, (i + step) % section_count) for i in range(section_count)]
        return lax.ppermute(value, "segment", pairs)

    gathered = exchanged(first_spread(members, blocks, inputs))
    gathered, *prepared = lax.optimization_barrier(
        (gathered, *prepare(exit_at, targets, repack, norm_gain, half, sub))
    )
    ranks, chunk_ranks, wanted, pick, sources, flags, gain = prepared
    parts, chunk, *weights = run_first_section(
        gathered, swapped(gathered), repack, gain, sub, (up_a, up_b, down_a, down_b)
    )
    kept, before = [], ()
    for section in range(3):
        if section:
            rows = exchanged(spread(members, chunk)).reshape(blocks, half, cols)
            kept.append(rows)
            parts, picked = run_section(section, rows, ranks, gain, pick, before, weights)
            before = (picked,)
        parts = exchanged(parts.reshape(members, sub, cols))
        chunk = hop(settle(section, parts, chunk, chunk_ranks), 1)
    head_sib = swapped(head)
    payload = run_payload(
        members, chunk, *kept, sources, wanted, exit_gain[None, :], head, head_sib
    )
    rows = exchanged(payload).reshape(blocks, half, cols)
    parts, mine, other, score, other_score = run_last_section(
        3, rows, ranks, gain, pick, picked, flags, weights
    )
    parts = exchanged(parts)
    selected = mine + swapped(other)
    score += swapped(other_score)
    selected, score = lax.optimization_barrier((selected, score))
    returned = hop(selected, -1)
    scores = score + hop(score, 1) + hop(score, 2) + hop(score, 3)
    return finish(3, parts, selected, returned, flags), scores[:, :1]


def solution(mesh):
    segments, groups, tensors = mesh.devices.shape
    fine = Mesh(
        mesh.devices.reshape(segments, groups, tensors // 2, 2), ("segment", "dp", "y", "core")
    )
    rows = ("dp", "y", "core")
    placed = (
        P(None, rows, None),
        P(),
        P(),
        P(),
        P("segment", None),
        P("segment", rows, None),
        P("segment", rows, None),
        P(),
        P(rows, None),
    )
    return jax.shard_map(
        on_device,
        mesh=fine,
        in_specs=placed,
        out_specs=(P("segment", None, rows, None), P(None, rows)),
        check_vma=False,
    )
```

```python
import functools

import jax
import jax.numpy as jnp
from jax import lax
from jax.experimental import pallas as pl
from jax.experimental.pallas import tpu as pltpu
from jax.sharding import Mesh, PartitionSpec as P

EPSILON = 1e-05
SQRT_HALF = 0.7071067811865476
FIRST_LIMIT = 39 * 1024 * 1024
SMALL_LIMIT = 4 * 1024 * 1024
WEIGHT_PARTS = 2
PLANE = ("dp", "y")
NT = (((1,), (1,)), ((), ()))
VMEM = pl.BlockSpec(memory_space=pltpu.VMEM)
SMEM = pl.BlockSpec(memory_space=pltpu.SMEM)
HBM = pl.BlockSpec(memory_space=pltpu.HBM)
SMALL = pltpu.CompilerParams(vmem_limit_bytes=SMALL_LIMIT)


def row_at(repack_ref, position):
    return repack_ref[0, 0, repack_ref[0, 1, position]]


def prepare_kernel(
    exit_ref, target_ref, repack_ref, gain_ref, rank_ref, chunk_rank_ref, wanted_ref, pick_ref,
    source_ref, flag_ref, ready_gain_ref
):
    half = rank_ref.shape[0]
    sub = chunk_rank_ref.shape[0]
    segment = lax.axis_index("segment")
    core = lax.axis_index("core")
    place = lax.axis_index("dp") * lax.axis_size("y") + lax.axis_index("y")
    first_row = lax.axis_index("y") * sub

    def source_of(position):
        first = repack_ref[0, 0, position]
        last = row_at(repack_ref, position)
        return jnp.where(segment == 3, last, jnp.where(segment == 2, first, position))

    mine = source_of(2 * place + core)
    other = source_of(2 * place + 1 - core)
    line = lax.broadcasted_iota(jnp.int32, (half, 1), 0)
    pick_line = lax.broadcasted_iota(jnp.int32, pick_ref.shape, 0)
    pick_lane = lax.broadcasted_iota(jnp.int32, pick_ref.shape, 1)
    ranks = jnp.zeros((half, 1), jnp.int32)
    wanteds = ranks
    sources = jnp.zeros(pick_ref.shape, jnp.int32)
    here, there = 0, 0
    for i in range(half):
        row = row_at(repack_ref, 2 * i + core)
        ranks = jnp.where(line == i, exit_ref[0, row], ranks)
        wanteds = jnp.where(line == i, target_ref[0, row], wanteds)
        sources = jnp.where(pick_lane == i, row, sources)
        here = jnp.where(row == 2 * place + core, 1, here)
        there = jnp.where(row == 2 * place + 1 - core, 1, there)
    rank_ref[...] = ranks
    wanted_ref[...] = wanteds
    source_ref[...] = sources
    ready_gain_ref[...] = gain_ref[...]
    pick_ref[...] = (
        ((pick_line == 0) & (sources == mine)) | ((pick_line == 1) & (sources == other))
    ).astype(jnp.float32)
    line = lax.broadcasted_iota(jnp.int32, (sub, 1), 0)
    ranks = jnp.zeros((sub, 1), jnp.int32)
    for i in range(sub):
        row = row_at(repack_ref, 2 * (first_row + i) + core)
        ranks = jnp.where(line == i, exit_ref[0, row], ranks)
    chunk_rank_ref[...] = ranks
    scoring = (segment >= 1) & (segment <= 2)
    chosen = scoring & (here == 1) & (exit_ref[0, 2 * place + core] == segment)
    other_chosen = scoring & (there == 1) & (exit_ref[0, 2 * place + 1 - core] == segment)
    rank = exit_ref[0, row_at(repack_ref, 2 * place + core)]
    living = (rank == 0) | (rank > 3)
    lines = lax.broadcasted_iota(jnp.int32, flag_ref.shape, 0)
    flag_ref[...] = (
        ((lines == 0) & chosen) | ((lines == 1) & other_chosen) | ((lines == 2) & living)
    ).astype(jnp.float32)


def prepare(exit_at, targets, repack, gain, half, sub):
    column = jax.ShapeDtypeStruct((half, 1), jnp.int32)
    return pl.pallas_call(
        prepare_kernel,
        out_shape=(
            column,
            jax.ShapeDtypeStruct((sub, 1), jnp.int32),
            column,
            jax.ShapeDtypeStruct((8, half), jnp.float32),
            jax.ShapeDtypeStruct((8, half), jnp.int32),
            jax.ShapeDtypeStruct((8, 128), jnp.float32),
            jax.ShapeDtypeStruct(gain.shape, gain.dtype),
        ),
        in_specs=[SMEM] * 3 + [VMEM],
        out_specs=(VMEM,) * 7,
        compiler_params=SMALL,
        name="prepare",
    )(exit_at, targets, repack, gain)


def normalise(rows_ref, gain_ref, living, out_ref):
    blocks, _, cols = rows_ref.shape
    width = blocks * cols
    total = rows_ref[0].astype(jnp.float32)
    for b in range(1, blocks):
        total += rows_ref[b].astype(jnp.float32)
    mean = jnp.sum(total, axis=1, keepdims=True) / width
    total = jnp.zeros_like(total)
    for b in range(blocks):
        lanes = slice(b * cols, (b + 1) * cols)
        center = rows_ref[b].astype(jnp.float32) - mean
        total += center * center
        out_ref[:, lanes] = (center * gain_ref[:, lanes]).astype(jnp.bfloat16)
    scale = lax.rsqrt(jnp.sum(total, axis=1, keepdims=True) / width + EPSILON)
    return scale if living is None else jnp.where(living, scale, 0.0)


def hidden_of(normed, scale, up_ref):
    pre = lax.dot_general(normed, up_ref[...], NT, preferred_element_type=jnp.float32) * scale
    return (0.5 * pre * (1.0 + lax.erf(pre * SQRT_HALF))).astype(jnp.bfloat16)


def project(hidden_a, hidden_b, down_a_ref, down_b_ref, out_ref, step=2):
    blocks, _, cols = out_ref.shape
    for b in range(0, blocks, step):
        lanes = slice(b * cols, (b + step) * cols)
        part = jnp.dot(hidden_a, down_a_ref[:, lanes], preferred_element_type=jnp.float32)
        part += jnp.dot(hidden_b, down_b_ref[:, lanes], preferred_element_type=jnp.float32)
        part = part.astype(jnp.bfloat16)
        for k in range(step):
            out_ref[b + k] = part[:, k * cols : (k + 1) * cols]


def pick_rows(section, rows_ref, pick_ref, before_ref, picked_ref):
    here = lax.axis_index("segment") == section

    def choose():
        pick = pick_ref[...].astype(jnp.bfloat16)
        for b in range(rows_ref.shape[0]):
            picked_ref[b] = jnp.dot(
                pick, rows_ref[b], preferred_element_type=jnp.float32
            ).astype(jnp.bfloat16)

    def keep():
        picked_ref[...] = before_ref[...]

    if before_ref is None:
        choose()
    else:
        pl.when(here)(choose)
        pl.when(jnp.logical_not(here))(keep)


def living_at(section, rank_ref):
    rank = rank_ref[...]
    return (rank == 0) | (rank > section)


def section_kernel(section, rows_ref, rank_ref, gain_ref, pick_ref, *refs):
    before_ref = refs[0] if len(refs) == 8 else None
    up_a_ref, up_b_ref, down_a_ref, down_b_ref, out_ref, picked_ref, normed_ref = refs[-7:]
    scale = normalise(rows_ref, gain_ref, living_at(section, rank_ref), normed_ref)
    normed = normed_ref[...]
    hidden_a = hidden_of(normed, scale, up_a_ref)
    hidden_b = hidden_of(normed, scale, up_b_ref)
    project(hidden_a, hidden_b, down_a_ref, down_b_ref, out_ref)
    pick_rows(section, rows_ref, pick_ref, before_ref, picked_ref)


def run_section(section, rows, ranks, gain, pick, before, weights):
    blocks, half, cols = rows.shape
    block = jax.ShapeDtypeStruct(rows.shape, jnp.bfloat16)
    hidden = 2 * weights[0].shape[0]
    return pl.pallas_call(
        functools.partial(section_kernel, section),
        out_shape=(block, jax.ShapeDtypeStruct((blocks, pick.shape[0], cols), jnp.bfloat16)),
        in_specs=[VMEM] * (8 + len(before)),
        out_specs=(VMEM, VMEM),
        scratch_shapes=[pltpu.VMEM((half, blocks * cols), jnp.bfloat16)],
        compiler_params=SMALL,
        cost_estimate=pl.CostEstimate(
            flops=4 * half * blocks * cols * hidden,
            bytes_accessed=4 * hidden * blocks * cols,
            transcendentals=half * hidden,
        ),
        name="section",
    )(rows, ranks, gain, pick, *before, *weights)


def settle_kernel(section, parts_ref, chunk_ref, *refs):
    out_ref = refs[-1]
    total = chunk_ref[...].astype(jnp.float32)
    if len(refs) == 2:
        total = jnp.where(living_at(section, refs[0]), total, 0.0)
    summed = parts_ref[0].astype(jnp.float32)
    for k in range(1, parts_ref.shape[0]):
        summed += parts_ref[k].astype(jnp.float32)
    out_ref[...] = (total + summed).astype(jnp.bfloat16)


def settle(section, parts, chunk, *chunk_ranks):
    return pl.pallas_call(
        functools.partial(settle_kernel, section),
        out_shape=jax.ShapeDtypeStruct(chunk.shape, jnp.bfloat16),
        in_specs=[VMEM] * (2 + len(chunk_ranks)),
        out_specs=VMEM,
        compiler_params=SMALL,
        name="settle",
    )(parts, chunk, *chunk_ranks)


def spread_kernel(chunk_ref, out_ref):
    chunk = chunk_ref[...]
    for k in range(out_ref.shape[0]):
        out_ref[k] = chunk


def spread(members, chunk):
    return pl.pallas_call(
        spread_kernel,
        out_shape=jax.ShapeDtypeStruct((members, *chunk.shape), jnp.bfloat16),
        in_specs=[VMEM],
        out_specs=VMEM,
        compiler_params=SMALL,
        name="spread",
    )(chunk)


def first_spread_kernel(row_ref, out_ref):
    members, blocks, cols = out_ref.shape
    row = row_ref[0].astype(jnp.float32)
    line = lax.broadcasted_iota(jnp.int32, (blocks, cols), 0)
    chunk = jnp.zeros((blocks, cols), jnp.float32)
    for b in range(blocks):
        chunk = jnp.where(line == b, row[:, b * cols : (b + 1) * cols], chunk)
    chunk = chunk.astype(jnp.bfloat16)
    for k in range(members):
        out_ref[k] = chunk


def first_spread(members, blocks, row):
    return pl.pallas_call(
        first_spread_kernel,
        out_shape=jax.ShapeDtypeStruct((members, blocks, row.shape[-1] // blocks), row.dtype),
        in_specs=[VMEM],
        out_specs=VMEM,
        compiler_params=SMALL,
        name="first_spread",
    )(row)


def copies_of(held_ref, ready_ref, sems, first, parts):
    rows = held_ref.shape[0] // parts
    return [
        pltpu.make_async_copy(
            held_ref.at[pl.ds(k * rows, rows)], ready_ref.at[pl.ds(k * rows, rows)], sems.at[first + k]
        )
        for k in range(parts)
    ]


def first_section_kernel(
    own_ref, sib_ref, repack_ref, gain_ref, up_b_ref, down_b_ref, held_up_ref, held_down_ref,
    out_ref, chunk_ref, up_a_ref, down_a_ref, gathered_ref, rows_ref, normed_ref, sems
):
    core = lax.axis_index("core")
    up_copies = copies_of(held_up_ref, up_a_ref, sems, 0, WEIGHT_PARTS)
    down_copies = copies_of(held_down_ref, down_a_ref, sems, WEIGHT_PARTS, WEIGHT_PARTS)
    for copy in up_copies + down_copies:
        copy.start()
    members, blocks, cols = gathered_ref.shape
    sub = chunk_ref.shape[0]
    for i in range(members):
        row = row_at(repack_ref, 2 * i + core)
        place = lax.shift_right_logical(row, 1)
        gathered_ref[i] = jnp.where(row & 1 == core, own_ref[place], sib_ref[place])
    rows = jnp.swapaxes(gathered_ref[...].astype(jnp.float32), 0, 1)
    rows_ref[...] = rows.astype(jnp.bfloat16)
    scale = normalise(rows_ref, gain_ref, None, normed_ref)
    block = lax.axis_index("dp")
    first_row = lax.axis_index("y") * sub
    line = lax.broadcasted_iota(jnp.int32, (blocks, cols), 0)
    chunk = jnp.zeros((sub, cols), jnp.float32)
    for r in range(sub):
        tile = gathered_ref[first_row + r].astype(jnp.float32)
        row = jnp.sum(jnp.where(line == block, tile, 0.0), axis=0, keepdims=True)
        chunk = jnp.where(line[:sub] == r, row, chunk)
    chunk_ref[...] = chunk.astype(jnp.bfloat16)
    normed = normed_ref[...]
    hidden_b = hidden_of(normed, scale, up_b_ref)
    for copy in up_copies:
        copy.wait()
    hidden_a = hidden_of(normed, scale, up_a_ref)
    for copy in down_copies:
        copy.wait()
    project(hidden_a, hidden_b, down_a_ref, down_b_ref, out_ref)


def run_first_section(own, sib, repack, gain, sub, weights):
    members, blocks, cols = own.shape
    shape = (blocks, members, cols)
    hidden = 2 * weights[0].shape[0]
    return pl.pallas_call(
        first_section_kernel,
        out_shape=(
            jax.ShapeDtypeStruct(shape, jnp.bfloat16),
            jax.ShapeDtypeStruct((sub, cols), jnp.bfloat16),
            *(jax.ShapeDtypeStruct(w.shape, w.dtype) for w in weights[2:]),
        ),
        in_specs=[VMEM, VMEM, SMEM] + [VMEM] * 3 + [HBM] * 2,
        out_specs=(VMEM,) * 4,
        scratch_shapes=[
            pltpu.VMEM(own.shape, jnp.bfloat16),
            pltpu.VMEM(shape, jnp.bfloat16),
            pltpu.VMEM((members, blocks * cols), jnp.bfloat16),
            pltpu.SemaphoreType.DMA((2 * WEIGHT_PARTS,)),
        ],
        compiler_params=pltpu.CompilerParams(vmem_limit_bytes=FIRST_LIMIT),
        cost_estimate=pl.CostEstimate(
            flops=4 * members * blocks * cols * hidden,
            bytes_accessed=4 * hidden * blocks * cols,
            transcendentals=members * hidden,
        ),
        name="first_section",
    )(own, sib, repack, gain, *weights)


def last_section_kernel(
    section, rows_ref, rank_ref, gain_ref, pick_ref, before_ref, flag_ref,
    up_a_ref, up_b_ref, down_a_ref, down_b_ref,
    out_ref, mine_ref, other_ref, score_ref, other_score_ref, normed_ref, picked_ref, parts_ref
):
    blocks, half, cols = rows_ref.shape
    core = lax.axis_index("core")

    @pl.when(lax.axis_index("segment") == section)
    def _():
        section_kernel(
            section, rows_ref, rank_ref, gain_ref, pick_ref, None,
            up_a_ref, up_b_ref, down_a_ref, down_b_ref, parts_ref, picked_ref, normed_ref
        )
        parts = jnp.swapaxes(parts_ref[...].astype(jnp.float32), 0, 1)
        out_ref[...] = parts.astype(jnp.bfloat16)

    @pl.when(lax.axis_index("segment") != section)
    def _():
        picked_ref[...] = before_ref[...]

    line = lax.broadcasted_iota(jnp.int32, (blocks, cols), 0)
    mine = jnp.zeros((blocks, cols), jnp.float32)
    other = mine
    for b in range(blocks):
        tile = picked_ref[b].astype(jnp.float32)
        mine = jnp.where(line == b, tile[0:1], mine)
        other = jnp.where(line == b, tile[1:2], other)
    mine_ref[...] = mine.astype(jnp.bfloat16)
    other_ref[...] = other.astype(jnp.bfloat16)
    sub = flag_ref.shape[0]
    sums = jnp.zeros(flag_ref.shape, jnp.float32)
    for b in range(blocks):
        for r in range(0, half, sub):
            sums += rows_ref[b, r : r + sub, :128].astype(jnp.float32)
    for index, ref in enumerate((score_ref, other_score_ref)):
        stats = jnp.where(core == index, sums[0:1], sums[1:2])
        exp_total = stats[:, 0:1] + stats[:, 2:3]
        picked = stats[:, 1:2] + stats[:, 3:4]
        flag = flag_ref[index : index + 1, 0:1]
        score = jnp.where(flag > 0.0, picked - jnp.log(exp_total), 0.0)
        ref[...] = jnp.broadcast_to(score, ref.shape)


def run_last_section(section, rows, ranks, gain, pick, before, flags, weights):
    blocks, half, cols = rows.shape
    hidden = 2 * weights[0].shape[0]
    row = jax.ShapeDtypeStruct((blocks, cols), jnp.bfloat16)
    score = jax.ShapeDtypeStruct((1, 128), jnp.float32)
    return pl.pallas_call(
        functools.partial(last_section_kernel, section),
        out_shape=(
            jax.ShapeDtypeStruct((half, blocks, cols), jnp.bfloat16), row, row, score, score
        ),
        in_specs=[VMEM] * 10,
        out_specs=(VMEM,) * 5,
        scratch_shapes=[
            pltpu.VMEM((half, blocks * cols), jnp.bfloat16),
            pltpu.VMEM(before.shape, jnp.bfloat16),
            pltpu.VMEM(rows.shape, jnp.bfloat16),
        ],
        compiler_params=SMALL,
        cost_estimate=pl.CostEstimate(
            flops=4 * half * blocks * cols * hidden,
            bytes_accessed=4 * hidden * blocks * cols,
            transcendentals=half * hidden,
        ),
        name="last_section",
    )(rows, ranks, gain, pick, before, flags, *weights)


def finish_kernel(section, parts_ref, row_ref, returned_ref, flag_ref, out_ref):
    blocks, cols = row_ref.shape
    here = lax.axis_index("segment") == section

    @pl.when(here)
    def _():
        total = jnp.where(flag_ref[2:3, 0:1] > 0.0, row_ref[...].astype(jnp.float32), 0.0)
        summed = parts_ref[0].astype(jnp.float32)
        for k in range(1, parts_ref.shape[0]):
            summed += parts_ref[k].astype(jnp.float32)
        total += summed
        for b in range(blocks):
            out_ref[0, 0, :, b * cols : (b + 1) * cols] = total[b : b + 1].astype(jnp.bfloat16)

    @pl.when(jnp.logical_not(here))
    def _():
        total = returned_ref[...].astype(jnp.float32)
        for b in range(blocks):
            out_ref[0, 0, :, b * cols : (b + 1) * cols] = total[b : b + 1].astype(jnp.bfloat16)


def finish(section, parts, row, returned, flags):
    width = row.shape[0] * row.shape[1]
    return pl.pallas_call(
        functools.partial(finish_kernel, section),
        out_shape=jax.ShapeDtypeStruct((1, 1, 1, width), jnp.bfloat16),
        in_specs=[VMEM] * 4,
        out_specs=VMEM,
        compiler_params=SMALL,
        name="finish",
    )(parts, row, returned, flags)


def payload_kernel(
    chunk_ref, first_ref, second_ref, source_ref, wanted_ref, gain_ref, head_a_ref, head_b_ref,
    out_ref, rows_ref, normed_ref
):
    members = out_ref.shape[0]
    segment = lax.axis_index("segment")
    core = lax.axis_index("core")
    place = lax.axis_index("dp") * lax.axis_size("y") + lax.axis_index("y")
    scoring = (segment >= 1) & (segment <= 2)

    @pl.when(jnp.logical_not(scoring))
    def _():
        chunk = chunk_ref[...]
        for k in range(members):
            out_ref[k] = chunk

    @pl.when(segment == 1)
    def _():
        rows_ref[...] = first_ref[...]

    @pl.when(segment == 2)
    def _():
        rows_ref[...] = second_ref[...]

    @pl.when(scoring)
    def _():
        scale = normalise(rows_ref, gain_ref, None, normed_ref)
        normed = normed_ref[...]
        half, vocab = normed.shape[0], head_a_ref.shape[0]
        wanted = wanted_ref[...]
        exp_part = jnp.zeros((half, 1), jnp.float32)
        picked = jnp.zeros((half, 1), jnp.float32)
        for ref, shard in (
            (head_a_ref, 2 * place + core),
            (head_b_ref, 2 * place + 1 - core),
        ):
            logits = lax.dot_general(normed, ref[...], NT, preferred_element_type=jnp.float32)
            logits *= scale
            exp_part += jnp.sum(jnp.exp(logits), axis=1, keepdims=True)
            columns = lax.broadcasted_iota(jnp.int32, logits.shape, 1) + shard * vocab
            picked += jnp.sum(jnp.where(columns == wanted, logits, 0.0), axis=1, keepdims=True)
        lane = lax.broadcasted_iota(jnp.int32, (half, 128), 1)
        both = jnp.where(lane % 2 == 0, exp_part, picked)
        high = both.astype(jnp.bfloat16).astype(jnp.float32)
        stats = jnp.where(lane < 2, high, jnp.where(lane < 4, both - high, 0.0))
        out_ref[...] = jnp.zeros_like(out_ref)
        stats = stats.astype(jnp.bfloat16)
        target = 2 * lax.broadcasted_iota(jnp.int32, (members, half), 0)
        sorted_stats = [
            jnp.dot(
                jnp.where(source_ref[0:1, :] == target + parity, 1.0, 0.0).astype(jnp.bfloat16),
                stats,
                preferred_element_type=jnp.float32,
            )
            for parity in range(2)
        ]
        line = lax.broadcasted_iota(jnp.int32, (out_ref.shape[1], 128), 0)
        for k in range(members):
            even, odd = (part[k : k + 1] for part in sorted_stats)
            tile = jnp.where(line == 0, even, jnp.where(line == 1, odd, 0.0))
            out_ref[k, :, :128] = tile.astype(jnp.bfloat16)


def run_payload(members, chunk, first, second, sources, wanted, gain, head_a, head_b):
    blocks, half, cols = first.shape
    return pl.pallas_call(
        payload_kernel,
        out_shape=jax.ShapeDtypeStruct((members, *chunk.shape), jnp.bfloat16),
        in_specs=[VMEM] * 8,
        out_specs=VMEM,
        scratch_shapes=[
            pltpu.VMEM(first.shape, jnp.bfloat16),
            pltpu.VMEM((half, blocks * cols), jnp.bfloat16),
        ],
        compiler_params=SMALL,
        name="payload",
    )(chunk, first, second, sources, wanted, gain, head_a, head_b)


def swapped(value):
    return lax.ppermute(value, "core", [(0, 1), (1, 0)])


def exchanged(value):
    return lax.all_to_all(value, PLANE, 0, 0, tiled=True)


def on_device(inputs, exit_at, targets, repack, norm_gain, up_weight, down_weight, exit_gain, head):
    section_count = lax.axis_size("segment")
    blocks = lax.axis_size("dp")
    y_count = lax.axis_size("y")
    members = blocks * y_count
    cols = inputs.shape[2] // blocks
    half = exit_at.shape[1] // 2
    sub = half // y_count
    up_a, down_a = up_weight[0], down_weight[0]
    up_b, down_b, head_sib = lax.optimization_barrier(
        (swapped(up_a), swapped(down_a), swapped(head))
    )

    def hop(value, step):
        pairs = [(i, (i + step) % section_count) for i in range(section_count)]
        return lax.ppermute(value, "segment", pairs)

    gathered = exchanged(first_spread(members, blocks, inputs))
    parts, chunk, up_a, down_a = run_first_section(
        gathered, swapped(gathered), repack, norm_gain, sub, (up_b, down_b, up_a, down_a)
    )
    weights = (up_a, up_b, down_a, down_b)
    parts = exchanged(parts.reshape(members, sub, cols))
    chunk = settle(0, parts, chunk)
    chunk, exit_at, targets, repack = lax.optimization_barrier((chunk, exit_at, targets, repack))
    chunk, *prepared = lax.optimization_barrier(
        (hop(chunk, 1), *prepare(exit_at, targets, repack, norm_gain, half, sub))
    )
    ranks, chunk_ranks, wanted, pick, sources, flags, gain = prepared
    kept, before = [], ()
    for section in (1, 2):
        rows = exchanged(spread(members, chunk)).reshape(blocks, half, cols)
        kept.append(rows)
        parts, picked = run_section(section, rows, ranks, gain, pick, before, weights)
        before = (picked,)
        parts = exchanged(parts.reshape(members, sub, cols))
        chunk = hop(settle(section, parts, chunk, chunk_ranks), 1)
    payload = run_payload(
        members, chunk, *kept, sources, wanted, exit_gain[None, :], head, head_sib
    )
    rows = exchanged(payload).reshape(blocks, half, cols)
    parts, mine, other, score, other_score = run_last_section(
        3, rows, ranks, gain, pick, picked, flags, weights
    )
    parts = exchanged(parts)
    selected = mine + swapped(other)
    score += swapped(other_score)
    selected, score = lax.optimization_barrier((selected, score))
    returned = hop(selected, -1)
    scores = score + hop(score, 1) + hop(score, 2) + hop(score, 3)
    return finish(3, parts, selected, returned, flags), scores[:, :1]


def solution(mesh):
    segments, groups, tensors = mesh.devices.shape
    fine = Mesh(
        mesh.devices.reshape(segments, groups, tensors // 2, 2), ("segment", "dp", "y", "core")
    )
    rows = ("dp", "y", "core")
    placed = (
        P(None, rows, None),
        P(),
        P(),
        P(),
        P("segment", None),
        P("segment", rows, None),
        P("segment", rows, None),
        P(),
        P(rows, None),
    )
    return jax.shard_map(
        on_device,
        mesh=fine,
        in_specs=placed,
        out_specs=(P("segment", None, rows, None), P(None, rows)),
        check_vma=False,
    )
```

```python
import functools

import jax
import jax.numpy as jnp
from jax import lax
from jax.experimental import pallas as pl
from jax.experimental.pallas import tpu as pltpu
from jax.sharding import Mesh, PartitionSpec as P

EPSILON = 1e-05
SQRT_HALF = 0.7071067811865476
FIRST_LIMIT = 39 * 1024 * 1024
SMALL_LIMIT = 4 * 1024 * 1024
WEIGHT_PARTS = 7
PLANE = ("dp", "y")
NT = (((1,), (1,)), ((), ()))
VMEM = pl.BlockSpec(memory_space=pltpu.VMEM)
SMEM = pl.BlockSpec(memory_space=pltpu.SMEM)
HBM = pl.BlockSpec(memory_space=pltpu.HBM)
SMALL = pltpu.CompilerParams(vmem_limit_bytes=SMALL_LIMIT)


def row_at(repack_ref, position):
    return repack_ref[0, 0, repack_ref[0, 1, position]]


def prepare_kernel(
    exit_ref, target_ref, repack_ref, gain_ref, rank_ref, chunk_rank_ref, wanted_ref, pick_ref,
    source_ref, flag_ref, ready_gain_ref
):
    half = rank_ref.shape[0]
    sub = chunk_rank_ref.shape[0]
    segment = lax.axis_index("segment")
    core = lax.axis_index("core")
    place = lax.axis_index("dp") * lax.axis_size("y") + lax.axis_index("y")
    first_row = lax.axis_index("y") * sub

    def source_of(position):
        first = repack_ref[0, 0, position]
        last = row_at(repack_ref, position)
        return jnp.where(segment == 3, last, jnp.where(segment == 2, first, position))

    mine = source_of(2 * place + core)
    other = source_of(2 * place + 1 - core)
    line = lax.broadcasted_iota(jnp.int32, (half, 1), 0)
    pick_line = lax.broadcasted_iota(jnp.int32, pick_ref.shape, 0)
    pick_lane = lax.broadcasted_iota(jnp.int32, pick_ref.shape, 1)
    ranks = jnp.zeros((half, 1), jnp.int32)
    wanteds = ranks
    sources = jnp.zeros(pick_ref.shape, jnp.int32)
    here, there = 0, 0
    for i in range(half):
        row = row_at(repack_ref, 2 * i + core)
        ranks = jnp.where(line == i, exit_ref[0, row], ranks)
        wanteds = jnp.where(line == i, target_ref[0, row], wanteds)
        sources = jnp.where(pick_lane == i, row, sources)
        here = jnp.where(row == 2 * place + core, 1, here)
        there = jnp.where(row == 2 * place + 1 - core, 1, there)
    rank_ref[...] = ranks
    wanted_ref[...] = wanteds
    source_ref[...] = sources
    ready_gain_ref[...] = gain_ref[...]
    pick_ref[...] = (
        ((pick_line == 0) & (sources == mine)) | ((pick_line == 1) & (sources == other))
    ).astype(jnp.float32)
    line = lax.broadcasted_iota(jnp.int32, (sub, 1), 0)
    ranks = jnp.zeros((sub, 1), jnp.int32)
    for i in range(sub):
        row = row_at(repack_ref, 2 * (first_row + i) + core)
        ranks = jnp.where(line == i, exit_ref[0, row], ranks)
    chunk_rank_ref[...] = ranks
    scoring = (segment >= 1) & (segment <= 2)
    chosen = scoring & (here == 1) & (exit_ref[0, 2 * place + core] == segment)
    other_chosen = scoring & (there == 1) & (exit_ref[0, 2 * place + 1 - core] == segment)
    rank = exit_ref[0, row_at(repack_ref, 2 * place + core)]
    living = (rank == 0) | (rank > 3)
    lines = lax.broadcasted_iota(jnp.int32, flag_ref.shape, 0)
    flag_ref[...] = (
        ((lines == 0) & chosen) | ((lines == 1) & other_chosen) | ((lines == 2) & living)
    ).astype(jnp.float32)


def prepare(exit_at, targets, repack, gain, half, sub):
    column = jax.ShapeDtypeStruct((half, 1), jnp.int32)
    return pl.pallas_call(
        prepare_kernel,
        out_shape=(
            column,
            jax.ShapeDtypeStruct((sub, 1), jnp.int32),
            column,
            jax.ShapeDtypeStruct((8, half), jnp.float32),
            jax.ShapeDtypeStruct((8, half), jnp.int32),
            jax.ShapeDtypeStruct((8, 128), jnp.float32),
            jax.ShapeDtypeStruct(gain.shape, gain.dtype),
        ),
        in_specs=[SMEM] * 3 + [VMEM],
        out_specs=(VMEM,) * 7,
        compiler_params=SMALL,
        name="prepare",
    )(exit_at, targets, repack, gain)


def normalise(rows_ref, gain_ref, living, out_ref):
    blocks, _, cols = rows_ref.shape
    width = blocks * cols
    total = rows_ref[0].astype(jnp.float32)
    for b in range(1, blocks):
        total += rows_ref[b].astype(jnp.float32)
    mean = jnp.sum(total, axis=1, keepdims=True) / width
    total = jnp.zeros_like(total)
    for b in range(blocks):
        lanes = slice(b * cols, (b + 1) * cols)
        center = rows_ref[b].astype(jnp.float32) - mean
        total += center * center
        out_ref[:, lanes] = (center * gain_ref[:, lanes]).astype(jnp.bfloat16)
    scale = lax.rsqrt(jnp.sum(total, axis=1, keepdims=True) / width + EPSILON)
    return scale if living is None else jnp.where(living, scale, 0.0)


def hidden_of(normed, scale, up_ref):
    pre = lax.dot_general(normed, up_ref[...], NT, preferred_element_type=jnp.float32) * scale
    return (0.5 * pre * (1.0 + lax.erf(pre * SQRT_HALF))).astype(jnp.bfloat16)


def project(hidden_a, hidden_b, down_a_ref, down_b_ref, out_ref, step=2):
    blocks, _, cols = out_ref.shape
    for b in range(0, blocks, step):
        lanes = slice(b * cols, (b + step) * cols)
        part = jnp.dot(hidden_a, down_a_ref[:, lanes], preferred_element_type=jnp.float32)
        part += jnp.dot(hidden_b, down_b_ref[:, lanes], preferred_element_type=jnp.float32)
        part = part.astype(jnp.bfloat16)
        for k in range(step):
            out_ref[b + k] = part[:, k * cols : (k + 1) * cols]


def pick_rows(section, rows_ref, pick_ref, before_ref, picked_ref):
    here = lax.axis_index("segment") == section

    def choose():
        pick = pick_ref[...].astype(jnp.bfloat16)
        for b in range(rows_ref.shape[0]):
            picked_ref[b] = jnp.dot(
                pick, rows_ref[b], preferred_element_type=jnp.float32
            ).astype(jnp.bfloat16)

    def keep():
        picked_ref[...] = before_ref[...]

    if before_ref is None:
        choose()
    else:
        pl.when(here)(choose)
        pl.when(jnp.logical_not(here))(keep)


def living_at(section, rank_ref):
    rank = rank_ref[...]
    return (rank == 0) | (rank > section)


def section_kernel(section, rows_ref, rank_ref, gain_ref, pick_ref, *refs):
    before_ref = refs[0] if len(refs) == 8 else None
    up_a_ref, up_b_ref, down_a_ref, down_b_ref, out_ref, picked_ref, normed_ref = refs[-7:]
    scale = normalise(rows_ref, gain_ref, living_at(section, rank_ref), normed_ref)
    normed = normed_ref[...]
    hidden_a = hidden_of(normed, scale, up_a_ref)
    hidden_b = hidden_of(normed, scale, up_b_ref)
    project(hidden_a, hidden_b, down_a_ref, down_b_ref, out_ref)
    pick_rows(section, rows_ref, pick_ref, before_ref, picked_ref)


def run_section(section, rows, ranks, gain, pick, before, weights):
    blocks, half, cols = rows.shape
    block = jax.ShapeDtypeStruct(rows.shape, jnp.bfloat16)
    hidden = 2 * weights[0].shape[0]
    return pl.pallas_call(
        functools.partial(section_kernel, section),
        out_shape=(block, jax.ShapeDtypeStruct((blocks, pick.shape[0], cols), jnp.bfloat16)),
        in_specs=[VMEM] * (8 + len(before)),
        out_specs=(VMEM, VMEM),
        scratch_shapes=[pltpu.VMEM((half, blocks * cols), jnp.bfloat16)],
        compiler_params=SMALL,
        cost_estimate=pl.CostEstimate(
            flops=4 * half * blocks * cols * hidden,
            bytes_accessed=4 * hidden * blocks * cols,
            transcendentals=half * hidden,
        ),
        name="section",
    )(rows, ranks, gain, pick, *before, *weights)


def settle_kernel(section, parts_ref, chunk_ref, *refs):
    out_ref = refs[-1]
    total = chunk_ref[...].astype(jnp.float32)
    if len(refs) == 2:
        total = jnp.where(living_at(section, refs[0]), total, 0.0)
    summed = parts_ref[0].astype(jnp.float32)
    for k in range(1, parts_ref.shape[0]):
        summed += parts_ref[k].astype(jnp.float32)
    out_ref[...] = (total + summed).astype(jnp.bfloat16)


def settle(section, parts, chunk, *chunk_ranks):
    return pl.pallas_call(
        functools.partial(settle_kernel, section),
        out_shape=jax.ShapeDtypeStruct(chunk.shape, jnp.bfloat16),
        in_specs=[VMEM] * (2 + len(chunk_ranks)),
        out_specs=VMEM,
        compiler_params=SMALL,
        name="settle",
    )(parts, chunk, *chunk_ranks)


def spread_kernel(chunk_ref, out_ref):
    chunk = chunk_ref[...]
    for k in range(out_ref.shape[0]):
        out_ref[k] = chunk


def spread(members, chunk):
    return pl.pallas_call(
        spread_kernel,
        out_shape=jax.ShapeDtypeStruct((members, *chunk.shape), jnp.bfloat16),
        in_specs=[VMEM],
        out_specs=VMEM,
        compiler_params=SMALL,
        name="spread",
    )(chunk)


def first_spread_kernel(row_ref, out_ref):
    members, blocks, cols = out_ref.shape
    row = row_ref[0].astype(jnp.float32)
    line = lax.broadcasted_iota(jnp.int32, (blocks, cols), 0)
    chunk = jnp.zeros((blocks, cols), jnp.float32)
    for b in range(blocks):
        chunk = jnp.where(line == b, row[:, b * cols : (b + 1) * cols], chunk)
    chunk = chunk.astype(jnp.bfloat16)
    for k in range(members):
        out_ref[k] = chunk


def first_spread(members, blocks, row):
    return pl.pallas_call(
        first_spread_kernel,
        out_shape=jax.ShapeDtypeStruct((members, blocks, row.shape[-1] // blocks), row.dtype),
        in_specs=[VMEM],
        out_specs=VMEM,
        compiler_params=SMALL,
        name="first_spread",
    )(row)


def copies_of(held_ref, ready_ref, sems, first, parts):
    rows = held_ref.shape[0] // parts
    return [
        pltpu.make_async_copy(
            held_ref.at[pl.ds(k * rows, rows)], ready_ref.at[pl.ds(k * rows, rows)], sems.at[first + k]
        )
        for k in range(parts)
    ]


def first_section_kernel(
    own_ref, sib_ref, repack_ref, gain_ref, up_b_ref, down_b_ref, held_up_ref, held_down_ref,
    out_ref, chunk_ref, up_a_ref, down_a_ref, gathered_ref, rows_ref, normed_ref, sems
):
    core = lax.axis_index("core")
    up_copies = copies_of(held_up_ref, up_a_ref, sems, 0, WEIGHT_PARTS)
    down_copies = copies_of(held_down_ref, down_a_ref, sems, WEIGHT_PARTS, WEIGHT_PARTS)
    for copy in up_copies:
        copy.start()
    members, blocks, cols = gathered_ref.shape
    sub = chunk_ref.shape[0]
    for i in range(members):
        row = row_at(repack_ref, 2 * i + core)
        place = lax.shift_right_logical(row, 1)
        gathered_ref[i] = jnp.where(row & 1 == core, own_ref[place], sib_ref[place])
    rows = jnp.swapaxes(gathered_ref[...].astype(jnp.float32), 0, 1)
    rows_ref[...] = rows.astype(jnp.bfloat16)
    for copy in down_copies:
        copy.start()
    scale = normalise(rows_ref, gain_ref, None, normed_ref)
    block = lax.axis_index("dp")
    first_row = lax.axis_index("y") * sub
    line = lax.broadcasted_iota(jnp.int32, (blocks, cols), 0)
    chunk = jnp.zeros((sub, cols), jnp.float32)
    for r in range(sub):
        tile = gathered_ref[first_row + r].astype(jnp.float32)
        row = jnp.sum(jnp.where(line == block, tile, 0.0), axis=0, keepdims=True)
        chunk = jnp.where(line[:sub] == r, row, chunk)
    chunk_ref[...] = chunk.astype(jnp.bfloat16)
    normed = normed_ref[...]
    hidden_b = hidden_of(normed, scale, up_b_ref)
    for copy in up_copies:
        copy.wait()
    hidden_a = hidden_of(normed, scale, up_a_ref)
    for copy in down_copies:
        copy.wait()
    project(hidden_a, hidden_b, down_a_ref, down_b_ref, out_ref)


def run_first_section(own, sib, repack, gain, sub, weights):
    members, blocks, cols = own.shape
    shape = (blocks, members, cols)
    hidden = 2 * weights[0].shape[0]
    return pl.pallas_call(
        first_section_kernel,
        out_shape=(
            jax.ShapeDtypeStruct(shape, jnp.bfloat16),
            jax.ShapeDtypeStruct((sub, cols), jnp.bfloat16),
            *(jax.ShapeDtypeStruct(w.shape, w.dtype) for w in weights[2:]),
        ),
        in_specs=[VMEM, VMEM, SMEM] + [VMEM] * 3 + [HBM] * 2,
        out_specs=(VMEM,) * 4,
        scratch_shapes=[
            pltpu.VMEM(own.shape, jnp.bfloat16),
            pltpu.VMEM(shape, jnp.bfloat16),
            pltpu.VMEM((members, blocks * cols), jnp.bfloat16),
            pltpu.SemaphoreType.DMA((2 * WEIGHT_PARTS,)),
        ],
        compiler_params=pltpu.CompilerParams(vmem_limit_bytes=FIRST_LIMIT),
        cost_estimate=pl.CostEstimate(
            flops=4 * members * blocks * cols * hidden,
            bytes_accessed=4 * hidden * blocks * cols,
            transcendentals=members * hidden,
        ),
        name="first_section",
    )(own, sib, repack, gain, *weights)


def last_section_kernel(
    section, rows_ref, rank_ref, gain_ref, pick_ref, before_ref, flag_ref,
    up_a_ref, up_b_ref, down_a_ref, down_b_ref,
    out_ref, mine_ref, other_ref, score_ref, other_score_ref, normed_ref, picked_ref, parts_ref
):
    blocks, half, cols = rows_ref.shape
    core = lax.axis_index("core")

    @pl.when(lax.axis_index("segment") == section)
    def _():
        section_kernel(
            section, rows_ref, rank_ref, gain_ref, pick_ref, None,
            up_a_ref, up_b_ref, down_a_ref, down_b_ref, parts_ref, picked_ref, normed_ref
        )
        parts = jnp.swapaxes(parts_ref[...].astype(jnp.float32), 0, 1)
        out_ref[...] = parts.astype(jnp.bfloat16)

    @pl.when(lax.axis_index("segment") != section)
    def _():
        picked_ref[...] = before_ref[...]

    line = lax.broadcasted_iota(jnp.int32, (blocks, cols), 0)
    mine = jnp.zeros((blocks, cols), jnp.float32)
    other = mine
    for b in range(blocks):
        tile = picked_ref[b].astype(jnp.float32)
        mine = jnp.where(line == b, tile[0:1], mine)
        other = jnp.where(line == b, tile[1:2], other)
    mine_ref[...] = mine.astype(jnp.bfloat16)
    other_ref[...] = other.astype(jnp.bfloat16)
    sub = flag_ref.shape[0]
    sums = jnp.zeros(flag_ref.shape, jnp.float32)
    for b in range(blocks):
        for r in range(0, half, sub):
            sums += rows_ref[b, r : r + sub, :128].astype(jnp.float32)
    for index, ref in enumerate((score_ref, other_score_ref)):
        stats = jnp.where(core == index, sums[0:1], sums[1:2])
        exp_total = stats[:, 0:1] + stats[:, 2:3]
        picked = stats[:, 1:2] + stats[:, 3:4]
        flag = flag_ref[index : index + 1, 0:1]
        score = jnp.where(flag > 0.0, picked - jnp.log(exp_total), 0.0)
        ref[...] = jnp.broadcast_to(score, ref.shape)


def run_last_section(section, rows, ranks, gain, pick, before, flags, weights):
    blocks, half, cols = rows.shape
    hidden = 2 * weights[0].shape[0]
    row = jax.ShapeDtypeStruct((blocks, cols), jnp.bfloat16)
    score = jax.ShapeDtypeStruct((1, 128), jnp.float32)
    return pl.pallas_call(
        functools.partial(last_section_kernel, section),
        out_shape=(
            jax.ShapeDtypeStruct((half, blocks, cols), jnp.bfloat16), row, row, score, score
        ),
        in_specs=[VMEM] * 10,
        out_specs=(VMEM,) * 5,
        scratch_shapes=[
            pltpu.VMEM((half, blocks * cols), jnp.bfloat16),
            pltpu.VMEM(before.shape, jnp.bfloat16),
            pltpu.VMEM(rows.shape, jnp.bfloat16),
        ],
        compiler_params=SMALL,
        cost_estimate=pl.CostEstimate(
            flops=4 * half * blocks * cols * hidden,
            bytes_accessed=4 * hidden * blocks * cols,
            transcendentals=half * hidden,
        ),
        name="last_section",
    )(rows, ranks, gain, pick, before, flags, *weights)


def finish_kernel(section, parts_ref, row_ref, returned_ref, flag_ref, out_ref):
    blocks, cols = row_ref.shape
    here = lax.axis_index("segment") == section

    @pl.when(here)
    def _():
        total = jnp.where(flag_ref[2:3, 0:1] > 0.0, row_ref[...].astype(jnp.float32), 0.0)
        summed = parts_ref[0].astype(jnp.float32)
        for k in range(1, parts_ref.shape[0]):
            summed += parts_ref[k].astype(jnp.float32)
        total += summed
        for b in range(blocks):
            out_ref[0, 0, :, b * cols : (b + 1) * cols] = total[b : b + 1].astype(jnp.bfloat16)

    @pl.when(jnp.logical_not(here))
    def _():
        total = returned_ref[...].astype(jnp.float32)
        for b in range(blocks):
            out_ref[0, 0, :, b * cols : (b + 1) * cols] = total[b : b + 1].astype(jnp.bfloat16)


def finish(section, parts, row, returned, flags):
    width = row.shape[0] * row.shape[1]
    return pl.pallas_call(
        functools.partial(finish_kernel, section),
        out_shape=jax.ShapeDtypeStruct((1, 1, 1, width), jnp.bfloat16),
        in_specs=[VMEM] * 4,
        out_specs=VMEM,
        compiler_params=SMALL,
        name="finish",
    )(parts, row, returned, flags)


def payload_kernel(
    chunk_ref, first_ref, second_ref, source_ref, wanted_ref, gain_ref, head_a_ref, head_b_ref,
    out_ref, rows_ref, normed_ref
):
    members = out_ref.shape[0]
    segment = lax.axis_index("segment")
    core = lax.axis_index("core")
    place = lax.axis_index("dp") * lax.axis_size("y") + lax.axis_index("y")
    scoring = (segment >= 1) & (segment <= 2)

    @pl.when(jnp.logical_not(scoring))
    def _():
        chunk = chunk_ref[...]
        for k in range(members):
            out_ref[k] = chunk

    @pl.when(segment == 1)
    def _():
        rows_ref[...] = first_ref[...]

    @pl.when(segment == 2)
    def _():
        rows_ref[...] = second_ref[...]

    @pl.when(scoring)
    def _():
        scale = normalise(rows_ref, gain_ref, None, normed_ref)
        normed = normed_ref[...]
        half, vocab = normed.shape[0], head_a_ref.shape[0]
        wanted = wanted_ref[...]
        exp_part = jnp.zeros((half, 1), jnp.float32)
        picked = jnp.zeros((half, 1), jnp.float32)
        for ref, shard in (
            (head_a_ref, 2 * place + core),
            (head_b_ref, 2 * place + 1 - core),
        ):
            logits = lax.dot_general(normed, ref[...], NT, preferred_element_type=jnp.float32)
            logits *= scale
            exp_part += jnp.sum(jnp.exp(logits), axis=1, keepdims=True)
            columns = lax.broadcasted_iota(jnp.int32, logits.shape, 1) + shard * vocab
            picked += jnp.sum(jnp.where(columns == wanted, logits, 0.0), axis=1, keepdims=True)
        lane = lax.broadcasted_iota(jnp.int32, (half, 128), 1)
        both = jnp.where(lane % 2 == 0, exp_part, picked)
        high = both.astype(jnp.bfloat16).astype(jnp.float32)
        stats = jnp.where(lane < 2, high, jnp.where(lane < 4, both - high, 0.0))
        out_ref[...] = jnp.zeros_like(out_ref)
        stats = stats.astype(jnp.bfloat16)
        target = 2 * lax.broadcasted_iota(jnp.int32, (members, half), 0)
        sorted_stats = [
            jnp.dot(
                jnp.where(source_ref[0:1, :] == target + parity, 1.0, 0.0).astype(jnp.bfloat16),
                stats,
                preferred_element_type=jnp.float32,
            )
            for parity in range(2)
        ]
        line = lax.broadcasted_iota(jnp.int32, (out_ref.shape[1], 128), 0)
        for k in range(members):
            even, odd = (part[k : k + 1] for part in sorted_stats)
            tile = jnp.where(line == 0, even, jnp.where(line == 1, odd, 0.0))
            out_ref[k, :, :128] = tile.astype(jnp.bfloat16)


def run_payload(members, chunk, first, second, sources, wanted, gain, head_a, head_b):
    blocks, half, cols = first.shape
    return pl.pallas_call(
        payload_kernel,
        out_shape=jax.ShapeDtypeStruct((members, *chunk.shape), jnp.bfloat16),
        in_specs=[VMEM] * 8,
        out_specs=VMEM,
        scratch_shapes=[
            pltpu.VMEM(first.shape, jnp.bfloat16),
            pltpu.VMEM((half, blocks * cols), jnp.bfloat16),
        ],
        compiler_params=SMALL,
        name="payload",
    )(chunk, first, second, sources, wanted, gain, head_a, head_b)


def swapped(value):
    return lax.ppermute(value, "core", [(0, 1), (1, 0)])


def exchanged(value):
    return lax.all_to_all(value, PLANE, 0, 0, tiled=True)


def on_device(inputs, exit_at, targets, repack, norm_gain, up_weight, down_weight, exit_gain, head):
    section_count = lax.axis_size("segment")
    blocks = lax.axis_size("dp")
    y_count = lax.axis_size("y")
    members = blocks * y_count
    cols = inputs.shape[2] // blocks
    half = exit_at.shape[1] // 2
    sub = half // y_count
    up_a, down_a = up_weight[0], down_weight[0]
    up_b, down_b, head_sib = lax.optimization_barrier(
        (swapped(up_a), swapped(down_a), swapped(head))
    )

    def hop(value, step):
        pairs = [(i, (i + step) % section_count) for i in range(section_count)]
        return lax.ppermute(value, "segment", pairs)

    gathered = exchanged(first_spread(members, blocks, inputs))
    parts, chunk, up_a, down_a = run_first_section(
        gathered, swapped(gathered), repack, norm_gain, sub, (up_b, down_b, up_a, down_a)
    )
    weights = (up_a, up_b, down_a, down_b)
    parts = exchanged(parts.reshape(members, sub, cols))
    chunk = settle(0, parts, chunk)
    chunk, exit_at, targets, repack = lax.optimization_barrier((chunk, exit_at, targets, repack))
    chunk, *prepared = lax.optimization_barrier(
        (hop(chunk, 1), *prepare(exit_at, targets, repack, norm_gain, half, sub))
    )
    ranks, chunk_ranks, wanted, pick, sources, flags, gain = prepared
    kept, before = [], ()
    for section in (1, 2):
        rows = exchanged(spread(members, chunk)).reshape(blocks, half, cols)
        kept.append(rows)
        parts, picked = run_section(section, rows, ranks, gain, pick, before, weights)
        before = (picked,)
        parts = exchanged(parts.reshape(members, sub, cols))
        chunk = hop(settle(section, parts, chunk, chunk_ranks), 1)
    payload = run_payload(
        members, chunk, *kept, sources, wanted, exit_gain[None, :], head, head_sib
    )
    rows = exchanged(payload).reshape(blocks, half, cols)
    parts, mine, other, score, other_score = run_last_section(
        3, rows, ranks, gain, pick, picked, flags, weights
    )
    parts = exchanged(parts)
    selected = mine + swapped(other)
    score += swapped(other_score)
    selected, score = lax.optimization_barrier((selected, score))
    returned = hop(selected, -1)
    scores = score + hop(score, 1) + hop(score, 2) + hop(score, 3)
    return finish(3, parts, selected, returned, flags), scores[:, :1]


def solution(mesh):
    segments, groups, tensors = mesh.devices.shape
    fine = Mesh(
        mesh.devices.reshape(segments, groups, tensors // 2, 2), ("segment", "dp", "y", "core")
    )
    rows = ("dp", "y", "core")
    placed = (
        P(None, rows, None),
        P(),
        P(),
        P(),
        P("segment", None),
        P("segment", rows, None),
        P("segment", rows, None),
        P(),
        P(rows, None),
    )
    return jax.shard_map(
        on_device,
        mesh=fine,
        in_specs=placed,
        out_specs=(P("segment", None, rows, None), P(None, rows)),
        check_vma=False,
    )
```
